32 devices in a mesh: win: 2 (over y), lon: 8 (over z, x), lat: 2 (over core).
Axes of the slice: x: 2, y: 2, z: 4, core: 2. Of those that a mesh axis runs over, the one named last changes fastest.
Arguments:
- dual_state: float32 [2, 16, 2, 4096], P('win', None, 'lat', 'lon'), may hold values from -6 to 6
- dual_obs: float32 [2, 16, 2, 4096], P('win', None, 'lat', 'lon'), may hold values from -6 to 6
- increment: float32 [2, 16, 2, 4096], P('win', None, 'lat', 'lon'), may hold values from -6 to 6
- resid_dual: float32 [2, 16, 2, 4096], P('win', None, 'lat', 'lon'), may hold values from -6 to 6
- resid_obs: float32 [2, 16, 2, 4096], P('win', None, 'lat', 'lon'), may hold values from -6 to 6
- resid_incr: float32 [2, 16, 2, 4096], P('win', None, 'lat', 'lon'), may hold values from -6 to 6
- search_dual: float32 [2, 16, 2, 4096], P('win', None, 'lat', 'lon'), may hold values from -6 to 6
- search_obs: float32 [2, 16, 2, 4096], P('win', None, 'lat', 'lon'), may hold values from -6 to 6
- search_incr: float32 [2, 16, 2, 4096], P('win', None, 'lat', 'lon'), may hold values from -6 to 6
- ensemble: bfloat16 [2, 64, 16, 2, 4096], P('win', None, None, 'lat', 'lon'), may hold values from -12 to 12
- tangent_coefs: float32 [2, 5, 16, 2, 4096], P('win', None, None, 'lat', 'lon'), may hold values from -0.25 to 0.25
- obs_weight: float32 [2, 16, 2, 4096], P('win', None, 'lat', 'lon'), may hold values from 0.25 to 2
- obs_var: float32 [2, 16, 2, 4096], P('win', None, 'lat', 'lon'), may hold values from 0.5 to 2
- loc_cols: int32 [8, 5], P('lon'), may hold values from 0 to 7, as said below
- loc_vals: bfloat16 [8, 5, 512, 512], P('lon'), may hold values from -0.125 to 0.125
Outputs:
- next_dual: float32 [2, 16, 2, 4096], P('win', None, 'lat', 'lon')
- next_obs: float32 [2, 16, 2, 4096], P('win', None, 'lat', 'lon')
- next_incr: float32 [2, 16, 2, 4096], P('win', None, 'lat', 'lon')
- next_res_dual: float32 [2, 16, 2, 4096], P('win', None, 'lat', 'lon')
- next_res_obs: float32 [2, 16, 2, 4096], P('win', None, 'lat', 'lon')
- next_res_incr: float32 [2, 16, 2, 4096], P('win', None, 'lat', 'lon')
The draws below stay inside these ranges and needn't reach their ends.
Inputs may be any that keep to these rules, and one draw needn't show every extreme that they name: `loc_cols`: row block i names 5 distinct column blocks, block i itself among them, each within 3 blocks of i around the longitude loop.
All inputs are finite; a program needn't handle non-finite values.
Results may differ from the reference program's by a relative error of at most 0.0017.
Values may be sent and summed in bfloat16 or wider, within the bound.
A program may use at most 64 MiB of HBM per device.

```python
import math
import jax
import jax.numpy as jnp
from jax import lax

LEV = 16
MEM = 64
BLK = 512
NB = 5
REACH = 3
NWIN = 2
NLAT = 2
NBLK = 8
NLON = 4096


def draw_loc_cols(key, part):
    keys = jax.random.split(key, NBLK)

    def one_row(row_key):
        first_key, second_key = jax.random.split(row_key)
        offsets = jnp.concatenate([jnp.arange(-REACH, 0, dtype=jnp.int32), jnp.arange(1, REACH + 1, dtype=jnp.int32)])
        picked = jax.random.permutation(first_key, offsets)[:NB - 1]
        chosen = jnp.concatenate([jnp.zeros((1,), jnp.int32), picked])
        return jax.random.permutation(second_key, chosen).astype(jnp.int32)
    offsets = jax.vmap(one_row)(keys)
    rows = jnp.arange(NBLK, dtype=jnp.int32)[:, None]
    return ((rows + offsets + NBLK) % NBLK).astype(jnp.int32)


def level_of(stream_key, dims, cuts, smallest, largest):
    def one(axis_at, blocks):
        draws = jax.random.uniform(jax.random.fold_in(jax.random.fold_in(stream_key, 6), axis_at), (blocks,), jnp.float32, smallest / len(cuts), largest / len(cuts))
        return jnp.repeat(jnp.exp(draws), dims[axis_at] // blocks).reshape((-1,) + (1,) * (len(dims) - axis_at - 1))

    gain = one(*cuts[0])
    for cut in cuts[1:]:
        gain = gain * one(*cut)
    return gain


def centred(rng, dims, width, limit, pieces=(), held_as=jnp.bfloat16):
    gain = level_of(rng, dims, pieces, -0.22, 0.18) if pieces else 1.0
    result = jax.random.normal(rng, dims, jnp.float32) * width * gain
    return jnp.minimum(jnp.maximum(result, -limit), limit).astype(held_as)


def setup_inputs(seed: int = 0) -> dict:
    key_of = jax.random.split(jax.random.key(seed), 16)
    return {
        "dual_state": centred(key_of[0], (NWIN, LEV, NLAT, NLON), 1.0, 6.0, ((0, 2), (2, 2), (3, 8)), jnp.float32),
        "dual_obs": centred(key_of[1], (NWIN, LEV, NLAT, NLON), 1.0, 6.0, ((0, 2), (2, 2), (3, 8)), jnp.float32),
        "increment": centred(key_of[2], (NWIN, LEV, NLAT, NLON), 1.0, 6.0, ((0, 2), (2, 2), (3, 8)), jnp.float32),
        "resid_dual": centred(key_of[3], (NWIN, LEV, NLAT, NLON), 1.0, 6.0, ((0, 2), (2, 2), (3, 8)), jnp.float32),
        "resid_obs": centred(key_of[4], (NWIN, LEV, NLAT, NLON), 1.0, 6.0, ((0, 2), (2, 2), (3, 8)), jnp.float32),
        "resid_incr": centred(key_of[5], (NWIN, LEV, NLAT, NLON), 1.0, 6.0, ((0, 2), (2, 2), (3, 8)), jnp.float32),
        "search_dual": centred(key_of[6], (NWIN, LEV, NLAT, NLON), 1.0, 6.0, ((0, 2), (2, 2), (3, 8)), jnp.float32),
        "search_obs": centred(key_of[7], (NWIN, LEV, NLAT, NLON), 1.0, 6.0, ((0, 2), (2, 2), (3, 8)), jnp.float32),
        "search_incr": centred(key_of[8], (NWIN, LEV, NLAT, NLON), 1.0, 6.0, ((0, 2), (2, 2), (3, 8)), jnp.float32),
        "ensemble": centred(key_of[9], (NWIN, MEM, LEV, NLAT, NLON), 2.0, 12.0, ((0, 2), (3, 2), (4, 8))),
        "tangent_coefs": jnp.clip(jax.random.uniform(key_of[10], (NWIN, 5, LEV, NLAT, NLON), jnp.float32, -0.25, 0.25) * level_of(key_of[10], (NWIN, 5, LEV, NLAT, NLON), ((0, 2), (3, 2), (4, 8)), -0.4, 0.0), -0.25, 0.25),
        "obs_weight": jnp.clip(jnp.exp(math.log(2.0) - 2.0794415 * jax.random.uniform(key_of[11], (NWIN, LEV, NLAT, NLON), jnp.float32) ** level_of(key_of[11], (NWIN, LEV, NLAT, NLON), ((0, 2), (2, 2), (3, 8)), -0.2, 0.2)), 0.25, 2.0),
        "obs_var": jnp.clip(jnp.exp(math.log(2.0) - 1.3862944 * jax.random.uniform(key_of[12], (NWIN, LEV, NLAT, NLON), jnp.float32) ** level_of(key_of[12], (NWIN, LEV, NLAT, NLON), ((0, 2), (2, 2), (3, 8)), -0.2, 0.2)), 0.5, 2.0),
        "loc_cols": draw_loc_cols(jax.random.fold_in(key_of[15], 71), 0),
        "loc_vals": centred(key_of[14], (NBLK, NB, BLK, BLK), (BLK * NB) ** -0.5, 0.125, ((0, 8),)),
    }


def east(field):
    return jnp.roll(field, -1, axis=-1)


def west(field):
    return jnp.roll(field, 1, axis=-1)


def north(field):
    return jnp.concatenate([field[..., 1:, :], jnp.zeros_like(field[..., :1, :])], axis=-2)


def south(field):
    return jnp.concatenate([jnp.zeros_like(field[..., :1, :]), field[..., :-1, :]], axis=-2)


def tangent(field, coefs):
    return ((0.5 + coefs[:, 0]) * field + coefs[:, 1] * east(field) + coefs[:, 2] * west(field)
            + coefs[:, 3] * north(field) + coefs[:, 4] * south(field))


def adjoint(field, coefs):
    return ((0.5 + coefs[:, 0]) * field + west(coefs[:, 1] * field) + east(coefs[:, 2] * field)
            + south(coefs[:, 3] * field) + north(coefs[:, 4] * field))


def reference(dual_state, dual_obs, increment, resid_dual, resid_obs, resid_incr,
              search_dual, search_obs, search_incr, ensemble, tangent_coefs,
              obs_weight, obs_var, loc_cols, loc_vals):
    moved = tangent(tangent(search_incr, tangent_coefs), tangent_coefs)
    backed = adjoint(adjoint(search_dual, tangent_coefs), tangent_coefs)
    prior = jnp.concatenate([jnp.zeros_like(moved[:1]), moved[:-1]], axis=0)
    later = jnp.concatenate([backed[1:], jnp.zeros_like(backed[:1])], axis=0)
    tiles = loc_vals.astype(jnp.float32)

    def localize(pair):
        members, search = pair
        products = (members.astype(jnp.float32) * search[None]).astype(jnp.bfloat16)
        blocks = products.reshape(MEM * LEV * NLAT, NBLK, BLK).astype(jnp.float32)
        spread = jnp.zeros(blocks.shape, jnp.float32)
        for column in range(NB):
            source = jnp.take(blocks, loc_cols[:, column], axis=1)
            spread = spread + jnp.einsum("rbq,bqp->rbp", source, tiles[:, column])
        spread = spread.reshape(MEM, LEV, NLAT, NLON)
        return jnp.sum(members.astype(jnp.float32) * spread, axis=0) / (MEM - 1)

    covar = lax.map(localize, (ensemble, search_dual))
    image_dual = covar + search_incr - prior
    image_obs = obs_var * search_obs + obs_weight * search_incr
    image_incr = search_dual - later + obs_weight * search_obs
    resid_sq = jnp.sum(resid_dual * resid_dual) + jnp.sum(resid_obs * resid_obs) + jnp.sum(resid_incr * resid_incr)
    search_sq = jnp.sum(search_dual * search_dual) + jnp.sum(search_obs * search_obs) + jnp.sum(search_incr * search_incr)
    alpha = resid_sq / (search_sq + 1e-6)
    return (dual_state + alpha * search_dual, dual_obs + alpha * search_obs, increment + alpha * search_incr,
            resid_dual - alpha * image_dual, resid_obs - alpha * image_obs, resid_incr - alpha * image_incr)
```

```python
import functools

import jax
import jax.numpy as jnp
from jax import lax
from jax.experimental import pallas as pl
from jax.experimental.pallas import tpu as pltpu
from jax.sharding import PartitionSpec as P

REACH = 3
CHUNKS = 8
LAG = 2
LANES = 128
MESH = pl.DeviceIdType.MESH
BF16 = jnp.bfloat16
F32 = jnp.float32


def remote(src, dst, send, recv, where):
    return pltpu.make_async_remote_copy(
        src_ref=src,
        dst_ref=dst,
        send_sem=send,
        recv_sem=recv,
        device_id=where,
        device_id_type=MESH,
    )


def kernel(
    sizes,
    dual_state, dual_obs, increment,
    resid_dual, resid_obs, resid_incr,
    search_dual, search_obs, search_incr,
    ens, coefs, obs_weight, obs_var, cols, vals,
    next_dual, next_obs, next_incr,
    next_res_dual, next_res_obs, next_res_incr,
    near, near_s, own_s, w_home, w_out, w_in,
    g_own, g_lat, g_left, g_right,
    part, part_lon, pair, part_col,
    moved, moved_in, acc, back, covar_flat,
    e_send, e_recv, s_send, s_recv, w_send, w_recv, f_send, f_recv,
    g_send, g_recv, a_send, a_recv, b_send, b_recv,
    m_send, m_recv, r_send, r_recv,
):
    wins, bands, lats, members, levels, block = sizes
    colors = wins * lats
    pieces = block // LANES
    rows = members * levels // CHUNKS
    group = rows // levels
    share = block // colors
    win = lax.axis_index("win")
    lon = lax.axis_index("lon")
    lat = lax.axis_index("lat")
    color = win * lats + lat

    def at(lon_step=0, other_lat=False, win_step=0):
        return {
            "win": lax.rem(win + win_step + wins, wins),
            "lon": lax.rem(lon + lon_step + bands, bands),
            "lat": 1 - lat if other_lat else lat,
        }

    def peer(step):
        index = lax.rem(color + step, colors)
        return index, {"win": index // lats, "lon": lon, "lat": lax.rem(index, lats)}

    barrier = pltpu.get_barrier_semaphore()
    greeted = [at(step) for step in range(1, bands)]
    greeted += [peer(step)[1] for step in range(1, colors)]
    greeted += [at(1, True), at(-1, True)]
    for where in greeted:
        pl.semaphore_signal(barrier, inc=1, device_id=where, device_id_type=MESH)

    def rows_of(ref, base):
        return [ref[pl.ds(base + j, levels, stride=pieces), :] for j in range(pieces)]

    flat = levels * pieces
    for j, (u, v) in enumerate(zip(rows_of(search_dual, 0), rows_of(search_incr, 0))):
        own_s[:, pl.ds(j * LANES, LANES)] = u
        g_own[0, :, pl.ds(j * LANES, LANES)] = v
        g_own[1, :, pl.ds(j * LANES, LANES)] = u
    for c in range(5):
        for j, value in enumerate(rows_of(coefs, c * flat)):
            g_own[2 + c, :, pl.ds(j * LANES, LANES)] = value

    resid_sq = jnp.sum(resid_dual[...] ** 2 + resid_obs[...] ** 2 + resid_incr[...] ** 2)
    search_sq = jnp.sum(search_dual[...] ** 2 + search_obs[...] ** 2 + search_incr[...] ** 2)
    first_row = lax.broadcasted_iota(jnp.int32, (8, LANES), 0) == 0
    part[...] = jnp.where(first_row, resid_sq, search_sq)
    part_lon[lon] = part[...]

    def slot_of(step):
        target = lax.rem(lon + step + bands, bands)
        slot = jnp.int32(0)
        found = jnp.int32(0)
        for j in range(vals.shape[0]):
            hit = cols[0, j] == target
            slot = jnp.where(hit, j, slot)
            found = jnp.where(hit, 1, found)
        return slot, found > 0

    mine = pl.ds(pl.multiple_of(color * share, share), share)
    for d in range(1, REACH + 1):
        slot, found = slot_of(d)
        w_out[d - 1] = jnp.where(found, vals[slot, mine, :], jnp.zeros((share, block), BF16))

    pl.semaphore_wait(barrier, len(greeted))

    started = []

    def go(copy):
        copy.start()
        started.append(copy)

    for d in range(1, REACH + 1):
        go(remote(own_s, near_s.at[d - 1], s_send.at[d - 1], s_recv.at[d - 1], at(d)))
    for step in range(1, bands):
        go(remote(part, part_lon.at[lon], a_send.at[step], a_recv.at[lon], at(step)))
    go(remote(g_own, g_lat, g_send.at[0], g_recv.at[0], at(0, True)))
    head = g_own.at[:, :, pl.ds(0, LANES)]
    tail = g_own.at[:, :, pl.ds(block - LANES, LANES)]
    for other in range(2):
        go(remote(tail, g_left.at[other], g_send.at[1 + other], g_recv.at[1 + other], at(1, other == 1)))
        go(remote(head, g_right.at[other], g_send.at[3 + other], g_recv.at[3 + other], at(-1, other == 1)))
    for d in range(1, REACH + 1):
        go(remote(w_out.at[d - 1], w_in.at[d - 1, mine], w_send.at[d - 1], w_recv.at[d - 1], at(d)))

    even = lax.rem(lon, 2) == 0

    def lines(t):
        return pl.ds(pl.multiple_of(t * rows, rows), rows)

    def two_on(t):
        return remote(ens.at[lines(t)], near.at[1, lines(t)], e_send.at[0, t], e_recv.at[0, t], at(2))

    def one_on_even(t):
        return remote(ens.at[lines(t)], near.at[0, lines(t)], e_send.at[1, t], e_recv.at[1, t], at(1))

    def one_on_odd(t):
        return remote(near.at[1, lines(t)], near.at[0, lines(t)], e_send.at[1, t], e_recv.at[1, t], at(-1))

    def three_on(t):
        return remote(near.at[0, lines(t)], near.at[2, lines(t)], e_send.at[2, t], e_recv.at[2, t], at(2))

    def first_sends(t, carry):
        two_on(t).start()

        @pl.when(even)
        def _():
            one_on_even(t).start()

        return carry

    lax.fori_loop(0, CHUNKS, first_sends, 0)

    for d in range(REACH + 1):
        slot, found = slot_of(-d)
        w_home[d] = jnp.where(found, vals[slot], jnp.zeros((block, block), BF16))
    acc[...] = jnp.zeros_like(acc)

    for step in range(1, bands):
        source = lax.rem(lon + step, bands)
        remote(part, part_lon.at[source], a_send.at[step], a_recv.at[source], at(0)).wait_recv()
    pair[...] = jnp.sum(part_lon[...], axis=0)
    part_col[color] = pair[...]
    for step in range(1, colors):
        _, where = peer(step)
        go(remote(pair, part_col.at[color], b_send.at[step], b_recv.at[color], where))

    remote(g_own, g_lat, g_send.at[0], g_recv.at[0], at(0)).wait_recv()
    for other in range(2):
        remote(tail, g_left.at[other], g_send.at[1 + other], g_recv.at[1 + other], at(0)).wait_recv()
        remote(head, g_right.at[other], g_send.at[3 + other], g_recv.at[3 + other], at(0)).wait_recv()

    def wide(k, other):
        middle = g_lat if other else g_own
        return jnp.concatenate([g_left[other, k], middle[k], g_right[other, k]], axis=1)

    span = block + 2 * LANES

    def east(x):
        return pltpu.roll(x, span - 1, 1)

    def west(x):
        return pltpu.roll(x, 1, 1)

    here = [wide(k, 0) for k in range(7)]
    over = [wide(k, 1) for k in range(7)]
    south_row = lat == 0
    cross = jnp.where(south_row, here[5], here[6])
    cross_over = jnp.where(south_row, over[6], over[5])

    def forward(v, beyond, c, between):
        return (0.5 + c[2]) * v + c[3] * east(v) + c[4] * west(v) + between * beyond

    def adjoint(u, beyond, c, between):
        return (0.5 + c[2]) * u + west(c[3] * u) + east(c[4] * u) + between * beyond

    once = forward(here[0], over[0], here, cross)
    once_over = forward(over[0], here[0], over, cross_over)
    twice = forward(once, once_over, here, cross)
    back_once = adjoint(here[1], over[1], here, cross_over)
    back_over = adjoint(over[1], here[1], over, cross)
    back_twice = adjoint(back_once, back_over, here, cross_over)
    for j in range(pieces):
        cut = slice((j + 1) * LANES, (j + 2) * LANES)
        moved[0, pl.ds(j, levels, stride=pieces), :] = twice[:, cut]
        moved[1, pl.ds(j, levels, stride=pieces), :] = back_twice[:, cut]
    for k, way in enumerate((1, -1)):
        go(remote(moved.at[k], moved_in.at[k], m_send.at[k], m_recv.at[k], at(0, False, way)))

    for d in range(1, REACH + 1):
        part_of = w_in.at[d - 1, mine]
        remote(w_out.at[d - 1], part_of, w_send.at[d - 1], w_recv.at[d - 1], at(0)).wait_recv()
        for step in range(1, colors):
            _, where = peer(step)
            go(remote(part_of, part_of, f_send.at[step, d - 1], f_recv.at[color, d - 1], where))
    for d in range(1, REACH + 1):
        remote(own_s, near_s.at[d - 1], s_send.at[d - 1], s_recv.at[d - 1], at(0)).wait_recv()

    def shares_in():
        for d in range(1, REACH + 1):
            for step in range(1, colors):
                source, where = peer(step)
                theirs = pl.ds(pl.multiple_of(source * share, share), share)
                spot = w_in.at[d - 1, theirs]
                remote(spot, spot, f_send.at[step, d - 1], f_recv.at[source, d - 1], where).wait_recv()

    def spread_of(t):
        def read(ref, search):
            member = ref[...].astype(F32).reshape(group, levels, block)
            product = (member * search[None]).astype(BF16).reshape(rows, block)
            return member, product

        def weigh(member, spread):
            return jnp.sum(member * spread.reshape(group, levels, block), axis=0)

        member, product = read(ens.at[lines(t)], own_s[...])
        total = jnp.dot(product, w_home[0], preferred_element_type=F32)
        for d in range(1, REACH + 1):
            far, far_product = read(near.at[d - 1, lines(t)], near_s[d - 1])
            total = total + jnp.dot(far_product, w_home[d], preferred_element_type=F32)
            acc[d] += weigh(far, jnp.dot(product, w_in[d - 1], preferred_element_type=F32))
        acc[0] += weigh(member, total)

    def step_of(t, carry):
        @pl.when(t < CHUNKS)
        def _():
            two_on(t).wait_recv()

            @pl.when(jnp.logical_not(even))
            def _():
                one_on_odd(t).start()

            one_on_even(t).wait_recv()
            three_on(t).start()

        @pl.when(t == LAG)
        def _():
            shares_in()

        @pl.when(t >= LAG)
        def _():
            three_on(t - LAG).wait_recv()
            spread_of(t - LAG)

        return carry

    lax.fori_loop(0, CHUNKS + LAG, step_of, 0)

    for d in range(1, REACH + 1):
        go(remote(acc.at[d], back.at[d - 1], r_send.at[d - 1], r_recv.at[d - 1], at(-d)))

    for step in range(1, colors):
        source, where = peer(step)
        remote(pair, part_col.at[source], b_send.at[step], b_recv.at[source], where).wait_recv()
    sums = jnp.sum(part_col[...], axis=0)
    alpha = sums[0:1, :] / (sums[1:2, :] + 1e-6)

    next_dual[...] = dual_state[...] + alpha * search_dual[...]
    next_obs[...] = dual_obs[...] + alpha * search_obs[...]
    next_incr[...] = increment[...] + alpha * search_incr[...]
    image_obs = obs_var[...] * search_obs[...] + obs_weight[...] * search_incr[...]
    next_res_obs[...] = resid_obs[...] - alpha * image_obs
    for k in range(2):
        remote(moved.at[k], moved_in.at[k], m_send.at[k], m_recv.at[k], at(0)).wait_recv()
    later = jnp.where(win < wins - 1, moved_in[1], 0.0)
    image_incr = search_dual[...] - later + obs_weight[...] * search_obs[...]
    next_res_incr[...] = resid_incr[...] - alpha * image_incr
    prior = jnp.where(win > 0, moved_in[0], 0.0)

    for d in range(1, REACH + 1):
        remote(acc.at[d], back.at[d - 1], r_send.at[d - 1], r_recv.at[d - 1], at(0)).wait_recv()
    covar = (acc[0] + back[0] + back[1] + back[2]) / (members - 1)
    for j in range(pieces):
        covar_flat[pl.ds(j, levels, stride=pieces), :] = covar[:, j * LANES:(j + 1) * LANES]
    image_dual = covar_flat[...] + search_incr[...] - prior
    next_res_dual[...] = resid_dual[...] - alpha * image_dual

    for copy in started:
        copy.wait_send()

    def sent(t, carry):
        two_on(t).wait_send()
        one_on_even(t).wait_send()
        three_on(t).wait_send()
        return carry

    lax.fori_loop(0, CHUNKS, sent, 0)


def local(wins, bands, lats, *args):
    fields = list(args)
    _, members, levels, _, block = args[9].shape
    flat = levels * block // LANES
    for k in (0, 1, 2, 3, 4, 5, 6, 7, 8, 11, 12):
        fields[k] = args[k].reshape(flat, LANES)
    fields[9] = args[9].reshape(members * levels, block)
    fields[10] = args[10].reshape(5 * flat, LANES)
    fields[14] = args[14][0]
    colors = wins * lats
    share = block // colors
    vmem = pl.BlockSpec(memory_space=pltpu.VMEM)
    specs = [vmem] * 15
    specs[13] = pl.BlockSpec(memory_space=pltpu.SMEM)
    dma = pltpu.SemaphoreType.DMA
    pairs = [(3, CHUNKS), (REACH,), (REACH,), (colors, REACH), (5,), (bands,), (colors,), (2,), (REACH,)]
    outs = pl.pallas_call(
        functools.partial(kernel, (wins, bands, lats, members, levels, block)),
        out_shape=[jax.ShapeDtypeStruct((flat, LANES), F32)] * 6,
        in_specs=specs,
        out_specs=[vmem] * 6,
        scratch_shapes=[
            pltpu.VMEM((REACH, members * levels, block), BF16),
            pltpu.VMEM((REACH, levels, block), F32),
            pltpu.VMEM((levels, block), F32),
            pltpu.VMEM((REACH + 1, block, block), BF16),
            pltpu.VMEM((REACH, share, block), BF16),
            pltpu.VMEM((REACH, block, block), BF16),
            pltpu.VMEM((7, levels, block), F32),
            pltpu.VMEM((7, levels, block), F32),
            pltpu.VMEM((2, 7, levels, LANES), F32),
            pltpu.VMEM((2, 7, levels, LANES), F32),
            pltpu.VMEM((8, LANES), F32),
            pltpu.VMEM((bands, 8, LANES), F32),
            pltpu.VMEM((8, LANES), F32),
            pltpu.VMEM((colors, 8, LANES), F32),
            pltpu.VMEM((2, flat, LANES), F32),
            pltpu.VMEM((2, flat, LANES), F32),
            pltpu.VMEM((REACH + 1, levels, block), F32),
            pltpu.VMEM((REACH, levels, block), F32),
            pltpu.VMEM((flat, LANES), F32),
        ] + [dma(shape) for shape in pairs for _ in range(2)],
        compiler_params=pltpu.CompilerParams(
            collective_id=0, has_side_effects=True, vmem_limit_bytes=40 * 1024 * 1024
        ),
    )(*fields)
    return tuple(out.reshape(args[0].shape) for out in outs)


def solution(mesh):
    wins, bands, lats = (mesh.shape[name] for name in ("win", "lon", "lat"))
    field = P("win", None, "lat", "lon")
    deep = P("win", None, None, "lat", "lon")
    return jax.shard_map(
        functools.partial(local, wins, bands, lats),
        mesh=mesh,
        in_specs=(field,) * 9 + (deep, deep, field, field, P("lon", None), P("lon", None, None, None)),
        out_specs=(field,) * 6,
        check_vma=False,
    )
```

```python
import functools

import jax
import jax.numpy as jnp
from jax import lax
from jax.experimental import pallas as pl
from jax.experimental.pallas import tpu as pltpu
from jax.sharding import PartitionSpec as P

CHUNKS = 8
EARLY = 2
WEIGHTS = 4
LAG = 3
LANES = 128
MESH = pl.DeviceIdType.MESH
BF16 = jnp.bfloat16
F32 = jnp.float32


def remote(src, dst, send, recv, where):
    return pltpu.make_async_remote_copy(
        src_ref=src,
        dst_ref=dst,
        send_sem=send,
        recv_sem=recv,
        device_id=where,
        device_id_type=MESH,
    )


def kernel(
    sizes,
    dual_state_h, dual_obs_h, increment_h,
    resid_dual_h, resid_obs_h, resid_incr_h,
    search_dual_h, search_obs_h, search_incr_h,
    ens_h, coefs_h, obs_weight_h, obs_var_h, cols, vals_h,
    out,
    dual_state, dual_obs, increment,
    resid_dual, resid_obs, resid_incr,
    search_dual, search_obs, search_incr,
    ens, coefs, obs_weight, obs_var, vals, load,
    near, hold, near_s, own_s, w_home, w_out, w_in,
    g_own, g_lat, g_edge, g_side,
    part, part_lon, pair, part_col,
    moved, moved_in, acc, back, covar_flat,
    e_send, e_recv, s_send, s_recv, w_send, w_recv, f_send, f_recv, h_send, h_recv,
    g_send, g_recv, a_send, a_recv, b_send, b_recv,
    m_send, m_recv, r_send, r_recv,
):
    wins, bands, lats, members, levels, block = sizes
    colors = wins * lats
    pieces = block // LANES
    flat = levels * pieces
    rows = members * levels // CHUNKS
    group = rows // levels
    share = block // colors
    win = lax.axis_index("win")
    lon = lax.axis_index("lon")
    lat = lax.axis_index("lat")
    color = win * lats + lat

    loads = [
        pltpu.make_async_copy(source, target, load.at[k])
        for k, (source, target) in enumerate((
            (search_dual_h, search_dual), (search_incr_h, search_incr), (coefs_h, coefs),
            (vals_h, vals), (ens_h, ens), (search_obs_h, search_obs),
            (resid_dual_h, resid_dual), (resid_obs_h, resid_obs), (resid_incr_h, resid_incr),
            (dual_state_h, dual_state), (dual_obs_h, dual_obs), (increment_h, increment),
            (obs_weight_h, obs_weight), (obs_var_h, obs_var),
        ))
    ]
    for copy in loads:
        copy.start()

    def at(lon_step=0, other_lat=False, win_step=0):
        return {
            "win": lax.rem(win + win_step + wins, wins),
            "lon": lax.rem(lon + lon_step + bands, bands),
            "lat": 1 - lat if other_lat else lat,
        }

    def peer(step):
        index = lax.rem(color + step, colors)
        return index, {"win": index // lats, "lon": lon, "lat": lax.rem(index, lats)}

    barrier = pltpu.get_barrier_semaphore()
    greeted = [at(step) for step in range(1, bands)]
    greeted += [peer(step)[1] for step in range(1, colors)]
    greeted += [at(1, True), at(-1, True)]
    for where in greeted:
        pl.semaphore_signal(barrier, inc=1, device_id=where, device_id_type=MESH)

    def rows_of(ref, base):
        return [ref[pl.ds(base + j, levels, stride=pieces), :] for j in range(pieces)]

    for copy in loads[:3]:
        copy.wait()
    for j, (u, v) in enumerate(zip(rows_of(search_dual, 0), rows_of(search_incr, 0))):
        own_s[:, pl.ds(j * LANES, LANES)] = u
        g_own[0, :, pl.ds(j * LANES, LANES)] = v
        g_own[1, :, pl.ds(j * LANES, LANES)] = u
    for c in range(5):
        for j, value in enumerate(rows_of(coefs, c * flat)):
            g_own[2 + c, :, pl.ds(j * LANES, LANES)] = value
    lane = lax.broadcasted_iota(jnp.int32, (levels, LANES), 1)
    lead = g_own[0, :, pl.ds(0, LANES)]
    last = pltpu.roll(g_own[0, :, pl.ds(block - LANES, LANES)], 2, 1)
    for k in range(1, 7):
        chosen = lane // 2 == k
        lead = jnp.where(chosen, pltpu.roll(g_own[k, :, pl.ds(0, LANES)], 2 * k, 1), lead)
        last = jnp.where(chosen, pltpu.roll(g_own[k, :, pl.ds(block - LANES, LANES)], 2 * k + 2, 1), last)
    g_edge[0] = last
    g_edge[1] = lead

    def slot_of(step):
        target = lax.rem(lon + step + bands, bands)
        slot = jnp.int32(0)
        found = jnp.int32(0)
        for j in range(vals.shape[0]):
            hit = cols[0, j] == target
            slot = jnp.where(hit, j, slot)
            found = jnp.where(hit, 1, found)
        return slot, found > 0

    mine = pl.ds(pl.multiple_of(color * share, share), share)
    loads[3].wait()
    for k, step in enumerate((1, 3, -2, -3)):
        slot, found = slot_of(step)
        w_out[k] = jnp.where(found, vals[slot, mine, :], jnp.zeros((share, block), BF16))
    loads[4].wait()

    pl.semaphore_wait(barrier, len(greeted))

    started = []

    def go(copy):
        copy.start()
        started.append(copy)

    ways = (1, -2)
    for k, way in enumerate(ways):
        go(remote(own_s, near_s.at[k], s_send.at[k], s_recv.at[k], at(way)))
        both = pl.ds(2 * k, 2)
        go(remote(w_out.at[both], w_in.at[both, mine], w_send.at[k], w_recv.at[k], at(way)))
    go(remote(g_own, g_lat, g_send.at[0], g_recv.at[0], at(0, True)))

    def edge(side, other):
        n = 1 + 2 * side + other
        way = 1 - 2 * side
        return remote(g_edge.at[side], g_side.at[side, other], g_send.at[n], g_recv.at[n], at(way, other == 1))

    for side in range(2):
        for other in range(2):
            go(edge(side, other))

    parity = lax.rem(lon, 2)
    even = parity == 0

    def lines(t):
        return pl.ds(pl.multiple_of(t * rows, rows), rows)

    def halves(t):
        return pl.ds(pl.multiple_of(t // 2 * rows, rows), rows)

    def to_west(t):
        return remote(ens.at[lines(t)], near.at[1, lines(t)], e_send.at[0, t], e_recv.at[0, t], at(-2))

    def to_east(t):
        return remote(ens.at[lines(t)], near.at[0, lines(t)], e_send.at[1, t], e_recv.at[1, t], at(1))

    def to_relay(t):
        way = 3 * lax.rem(t, 2) - 1
        return remote(ens.at[lines(t)], hold.at[halves(t)], e_send.at[1, t], e_recv.at[2, t], at(way))

    def from_relay(t):
        return remote(hold.at[halves(t)], near.at[0, lines(t)], e_send.at[2, t], e_recv.at[1, t], at(2 - 3 * parity))

    def first_sends(t, carry):
        @pl.when(lat == 0)
        def _():
            to_west(t).start()

        @pl.when(even)
        def _():
            to_east(t).start()

        @pl.when(jnp.logical_not(even))
        def _():
            to_relay(t).start()

        @pl.when(lat != 0)
        def _():
            to_west(t).start()

        return carry

    lax.fori_loop(0, EARLY, first_sends, 0)

    for copy in loads[5:]:
        copy.wait()
    resid_sq = jnp.sum(resid_dual[...] ** 2 + resid_obs[...] ** 2 + resid_incr[...] ** 2)
    search_sq = jnp.sum(search_dual[...] ** 2 + search_obs[...] ** 2 + search_incr[...] ** 2)
    first_row = lax.broadcasted_iota(jnp.int32, (8, LANES), 0) == 0
    part[...] = jnp.where(first_row, resid_sq, search_sq)
    part_lon[lon] = part[...]
    for step in range(1, bands):
        go(remote(part, part_lon.at[lon], a_send.at[step], a_recv.at[lon], at(step)))

    for d, step in enumerate((0, -1, 2)):
        slot, found = slot_of(step)
        w_home[d] = jnp.where(found, vals[slot], jnp.zeros((block, block), BF16))
    acc[...] = jnp.zeros_like(acc)

    every = pl.ds(0, WEIGHTS)
    for k in range(2):
        both = pl.ds(2 * k, 2)
        remote(w_out.at[both], w_in.at[both, mine], w_send.at[k], w_recv.at[k], at(0)).wait_recv()
    spot = w_in.at[every, mine]
    for step in range(1, wins):
        go(remote(spot, spot, f_send.at[step], f_recv.at[win], at(0, False, step)))
    lax.fori_loop(EARLY, 2 * EARLY, first_sends, 0)

    remote(g_own, g_lat, g_send.at[0], g_recv.at[0], at(0)).wait_recv()
    for side in range(2):
        for other in range(2):
            edge(side, other).wait_recv()

    def wide(k, other):
        middle = g_lat if other else g_own
        before = pltpu.roll(g_side[0, other], LANES - 2 - 2 * k, 1)
        after = pltpu.roll(g_side[1, other], (LANES - 2 * k) % LANES, 1)
        return jnp.concatenate([before, middle[k], after], axis=1)

    span = block + 2 * LANES

    def east(x):
        return pltpu.roll(x, span - 1, 1)

    def west(x):
        return pltpu.roll(x, 1, 1)

    here = [wide(k, 0) for k in range(7)]
    over = [wide(k, 1) for k in range(7)]
    south_row = lat == 0
    cross = jnp.where(south_row, here[5], here[6])
    cross_over = jnp.where(south_row, over[6], over[5])

    def forward(v, beyond, c, between):
        return (0.5 + c[2]) * v + c[3] * east(v) + c[4] * west(v) + between * beyond

    def adjoint(u, beyond, c, between):
        return (0.5 + c[2]) * u + west(c[3] * u) + east(c[4] * u) + between * beyond

    once = forward(here[0], over[0], here, cross)
    once_over = forward(over[0], here[0], over, cross_over)
    twice = forward(once, once_over, here, cross)
    back_once = adjoint(here[1], over[1], here, cross_over)
    back_over = adjoint(over[1], here[1], over, cross)
    back_twice = adjoint(back_once, back_over, here, cross_over)
    for j in range(pieces):
        cut = slice((j + 1) * LANES, (j + 2) * LANES)
        moved[0, pl.ds(j, levels, stride=pieces), :] = twice[:, cut]
        moved[1, pl.ds(j, levels, stride=pieces), :] = back_twice[:, cut]
    for k, way in enumerate((1, -1)):
        go(remote(moved.at[k], moved_in.at[k], m_send.at[k], m_recv.at[k], at(0, False, way)))

    for step in range(1, bands):
        source = lax.rem(lon + step, bands)
        remote(part, part_lon.at[source], a_send.at[step], a_recv.at[source], at(0)).wait_recv()
    pair[...] = jnp.sum(part_lon[...], axis=0)
    part_col[color] = pair[...]
    for step in range(1, colors):
        _, where = peer(step)
        go(remote(pair, part_col.at[color], b_send.at[step], b_recv.at[color], where))

    for step in range(1, wins):
        source = lax.rem(win + step, wins)
        remote(spot, spot, f_send.at[step], f_recv.at[source], at(0)).wait_recv()

    def over_lat(w, holder):
        theirs = pl.ds(pl.multiple_of((w * lats + holder) * share, share), share)
        place = w_in.at[every, theirs]
        return remote(place, place, h_send.at[w], h_recv.at[w], at(0, True))

    for w in range(wins):
        go(over_lat(w, lat))
    lax.fori_loop(2 * EARLY, CHUNKS, first_sends, 0)
    for k in range(2):
        remote(own_s, near_s.at[k], s_send.at[k], s_recv.at[k], at(0)).wait_recv()

    def spread_of(t):
        def read(ref, search):
            member = ref[...].astype(F32).reshape(group, levels, block)
            product = (member * search[None]).astype(BF16).reshape(rows, block)
            return member, product

        def weigh(member, terms):
            total = sum(jnp.dot(p, w, preferred_element_type=F32) for p, w in terms)
            return jnp.sum(member * total.reshape(group, levels, block), axis=0)

        member, product = read(ens.at[lines(t)], own_s[...])
        first, first_product = read(near.at[0, lines(t)], near_s[0])
        second, second_product = read(near.at[1, lines(t)], near_s[1])
        acc[0] += weigh(member, ((product, w_home[0]), (first_product, w_home[1]), (second_product, w_home[2])))
        acc[1] += weigh(first, ((product, w_in[0]), (second_product, w_in[1])))
        acc[2] += weigh(second, ((product, w_in[2]), (first_product, w_in[3])))

    def step_of(t, carry):
        @pl.when(jnp.logical_and(t < CHUNKS, lax.rem(t, 2) == parity))
        def _():
            to_relay(t).wait_recv()
            from_relay(t).start()

        @pl.when(t == LAG)
        def _():
            for w in range(wins):
                over_lat(w, 1 - lat).wait_recv()

        @pl.when(t >= LAG)
        def _():
            to_west(t - LAG).wait_recv()
            to_east(t - LAG).wait_recv()
            spread_of(t - LAG)

        return carry

    lax.fori_loop(0, CHUNKS + LAG, step_of, 0)

    for k, way in enumerate(ways):
        go(remote(acc.at[1 + k], back.at[k], r_send.at[k], r_recv.at[k], at(-way)))

    for step in range(1, colors):
        source, where = peer(step)
        remote(pair, part_col.at[source], b_send.at[step], b_recv.at[source], where).wait_recv()
    sums = jnp.sum(part_col[...], axis=0)
    alpha = sums[0:1, :] / (sums[1:2, :] + 1e-6)

    out[0] = dual_state[...] + alpha * search_dual[...]
    out[1] = dual_obs[...] + alpha * search_obs[...]
    out[2] = increment[...] + alpha * search_incr[...]
    image_obs = obs_var[...] * search_obs[...] + obs_weight[...] * search_incr[...]
    out[4] = resid_obs[...] - alpha * image_obs
    for k in range(2):
        remote(moved.at[k], moved_in.at[k], m_send.at[k], m_recv.at[k], at(0)).wait_recv()
    later = jnp.where(win < wins - 1, moved_in[1], 0.0)
    image_incr = search_dual[...] - later + obs_weight[...] * search_obs[...]
    out[5] = resid_incr[...] - alpha * image_incr
    prior = jnp.where(win > 0, moved_in[0], 0.0)

    for k in range(2):
        remote(acc.at[1 + k], back.at[k], r_send.at[k], r_recv.at[k], at(0)).wait_recv()
    covar = (acc[0] + back[0] + back[1]) / (members - 1)
    for j in range(pieces):
        covar_flat[pl.ds(j, levels, stride=pieces), :] = covar[:, j * LANES:(j + 1) * LANES]
    image_dual = covar_flat[...] + search_incr[...] - prior
    out[3] = resid_dual[...] - alpha * image_dual

    for copy in started:
        copy.wait_send()

    def sent(t, carry):
        to_west(t).wait_send()
        to_east(t).wait_send()

        @pl.when(lax.rem(t, 2) == parity)
        def _():
            from_relay(t).wait_send()

        return carry

    lax.fori_loop(0, CHUNKS, sent, 0)


def local(wins, bands, lats, *args):
    fields = list(args)
    _, members, levels, _, block = args[9].shape
    flat = levels * block // LANES
    for k in (0, 1, 2, 3, 4, 5, 6, 7, 8, 11, 12):
        fields[k] = args[k].reshape(flat, LANES)
    fields[9] = args[9].reshape(members * levels, block)
    fields[10] = args[10].reshape(5 * flat, LANES)
    fields[14] = args[14][0]
    colors = wins * lats
    share = block // colors
    total = members * levels
    vmem = pl.BlockSpec(memory_space=pltpu.VMEM)
    specs = [pl.BlockSpec(memory_space=pl.ANY)] * 15
    specs[13] = pl.BlockSpec(memory_space=pltpu.SMEM)
    dma = pltpu.SemaphoreType.DMA
    pairs = [(3, CHUNKS), (2,), (2,), (wins,), (wins,), (5,), (bands,), (colors,), (2,), (2,)]
    out = pl.pallas_call(
        functools.partial(kernel, (wins, bands, lats, members, levels, block)),
        out_shape=jax.ShapeDtypeStruct((6, flat, LANES), F32),
        in_specs=specs,
        out_specs=vmem,
        scratch_shapes=[
            pltpu.VMEM(fields[k].shape, fields[k].dtype) for k in range(15) if k != 13
        ] + [
            dma((14,)),
            pltpu.VMEM((2, total, block), BF16),
            pltpu.VMEM((total // 2, block), BF16),
            pltpu.VMEM((2, levels, block), F32),
            pltpu.VMEM((levels, block), F32),
            pltpu.VMEM((3, block, block), BF16),
            pltpu.VMEM((WEIGHTS, share, block), BF16),
            pltpu.VMEM((WEIGHTS, block, block), BF16),
            pltpu.VMEM((7, levels, block), F32),
            pltpu.VMEM((7, levels, block), F32),
            pltpu.VMEM((2, levels, LANES), F32),
            pltpu.VMEM((2, 2, levels, LANES), F32),
            pltpu.VMEM((8, LANES), F32),
            pltpu.VMEM((bands, 8, LANES), F32),
            pltpu.VMEM((8, LANES), F32),
            pltpu.VMEM((colors, 8, LANES), F32),
            pltpu.VMEM((2, flat, LANES), F32),
            pltpu.VMEM((2, flat, LANES), F32),
            pltpu.VMEM((3, levels, block), F32),
            pltpu.VMEM((2, levels, block), F32),
            pltpu.VMEM((flat, LANES), F32),
        ] + [dma(shape) for shape in pairs for _ in range(2)],
        compiler_params=pltpu.CompilerParams(
            collective_id=0, has_side_effects=True, vmem_limit_bytes=60 * 1024 * 1024
        ),
    )(*fields)
    return tuple(out[k].reshape(args[0].shape) for k in range(6))


def solution(mesh):
    wins, bands, lats = (mesh.shape[name] for name in ("win", "lon", "lat"))
    field = P("win", None, "lat", "lon")
    deep = P("win", None, None, "lat", "lon")
    return jax.shard_map(
        functools.partial(local, wins, bands, lats),
        mesh=mesh,
        in_specs=(field,) * 9 + (deep, deep, field, field, P("lon", None), P("lon", None, None, None)),
        out_specs=(field,) * 6,
        check_vma=False,
    )
```

```python
import functools

import jax
import jax.numpy as jnp
from jax import lax
from jax.experimental import pallas as pl
from jax.experimental.pallas import tpu as pltpu
from jax.sharding import PartitionSpec as P

CHUNKS = 8
EARLY = 2
WEIGHTS = 4
LAG = 3
LANES = 128
MESH = pl.DeviceIdType.MESH
BF16 = jnp.bfloat16
F32 = jnp.float32


def remote(src, dst, send, recv, where):
    return pltpu.make_async_remote_copy(
        src_ref=src,
        dst_ref=dst,
        send_sem=send,
        recv_sem=recv,
        device_id=where,
        device_id_type=MESH,
    )


def kernel(
    sizes,
    dual_state_h, dual_obs_h, increment_h,
    resid_dual_h, resid_obs_h, resid_incr_h,
    search_dual_h, search_obs_h, search_incr_h,
    ens_h, coefs_h, obs_weight_h, obs_var_h, cols, vals_h,
    out,
    dual_state, dual_obs, increment,
    resid_dual, resid_obs, resid_incr,
    search_dual, search_obs, search_incr,
    ens, coefs, obs_weight, obs_var, vals, load,
    near, hold, near_s, own_s, w_home, w_out, w_in,
    g_own, g_lat, g_edge, g_side,
    part, part_lon, pair, part_col,
    moved, moved_in, acc, back, covar_flat,
    e_send, e_recv, s_send, s_recv, w_send, w_recv, f_send, f_recv, h_send, h_recv,
    g_send, g_recv, a_send, a_recv, b_send, b_recv,
    m_send, m_recv, r_send, r_recv,
):
    wins, bands, lats, members, levels, block = sizes
    colors = wins * lats
    pieces = block // LANES
    flat = levels * pieces
    rows = members * levels // CHUNKS
    group = rows // levels
    share = block // colors
    win = lax.axis_index("win")
    lon = lax.axis_index("lon")
    lat = lax.axis_index("lat")
    color = win * lats + lat

    def at(lon_step=0, other_lat=False, win_step=0):
        return {
            "win": lax.rem(win + win_step + wins, wins),
            "lon": lax.rem(lon + lon_step + bands, bands),
            "lat": 1 - lat if other_lat else lat,
        }

    def peer(step):
        index = lax.rem(color + step, colors)
        return index, {"win": index // lats, "lon": lon, "lat": lax.rem(index, lats)}

    barrier = pltpu.get_barrier_semaphore()
    greeted = [at(step) for step in range(1, bands)]
    greeted += [peer(step)[1] for step in range(1, colors)]
    greeted += [at(1, True), at(-1, True)]
    for where in greeted:
        pl.semaphore_signal(barrier, inc=1, device_id=where, device_id_type=MESH)

    loads = [
        pltpu.make_async_copy(source, target, load.at[k])
        for k, (source, target) in enumerate((
            (ens_h, ens), (search_dual_h, search_dual), (search_incr_h, search_incr),
            (vals_h, vals), (coefs_h, coefs), (search_obs_h, search_obs),
            (resid_dual_h, resid_dual), (resid_obs_h, resid_obs), (resid_incr_h, resid_incr),
            (dual_state_h, dual_state), (dual_obs_h, dual_obs), (increment_h, increment),
            (obs_weight_h, obs_weight), (obs_var_h, obs_var),
        ))
    ]
    for copy in loads:
        copy.start()

    started = []

    def go(copy):
        copy.start()
        started.append(copy)

    parity = lax.rem(lon, 2)
    even = parity == 0

    def lines(t):
        return pl.ds(pl.multiple_of(t * rows, rows), rows)

    def halves(t):
        return pl.ds(pl.multiple_of(t // 2 * rows, rows), rows)

    def to_west(t):
        return remote(ens.at[lines(t)], near.at[1, lines(t)], e_send.at[0, t], e_recv.at[0, t], at(-2))

    def to_east(t):
        return remote(ens.at[lines(t)], near.at[0, lines(t)], e_send.at[1, t], e_recv.at[1, t], at(1))

    def to_relay(t):
        way = 3 * lax.rem(t, 2) - 1
        return remote(ens.at[lines(t)], hold.at[halves(t)], e_send.at[1, t], e_recv.at[2, t], at(way))

    def from_relay(t):
        return remote(hold.at[halves(t)], near.at[0, lines(t)], e_send.at[2, t], e_recv.at[1, t], at(2 - 3 * parity))

    def first_sends(t, carry):
        direct_first = jnp.logical_and(lat == 0, t < CHUNKS // 2)

        @pl.when(direct_first)
        def _():
            to_west(t).start()

        @pl.when(even)
        def _():
            to_east(t).start()

        @pl.when(jnp.logical_not(even))
        def _():
            to_relay(t).start()

        @pl.when(jnp.logical_not(direct_first))
        def _():
            to_west(t).start()

        return carry

    def relayed(t, carry):
        @pl.when(lax.rem(t, 2) == parity)
        def _():
            to_relay(t).wait_recv()
            from_relay(t).start()

        return carry

    loads[0].wait()
    pl.semaphore_wait(barrier, len(greeted))
    lax.fori_loop(0, EARLY, first_sends, 0)

    def slot_of(step):
        target = lax.rem(lon + step + bands, bands)
        slot = jnp.int32(0)
        found = jnp.int32(0)
        for j in range(vals.shape[0]):
            hit = cols[0, j] == target
            slot = jnp.where(hit, j, slot)
            found = jnp.where(hit, 1, found)
        return slot, found > 0

    mine = pl.ds(pl.multiple_of(color * share, share), share)
    loads[3].wait()
    for k, step in enumerate((1, 3, -2, -3)):
        slot, found = slot_of(step)
        w_out[k] = jnp.where(found, vals[slot, mine, :], jnp.zeros((share, block), BF16))

    def rows_of(ref, base):
        return [ref[pl.ds(base + j, levels, stride=pieces), :] for j in range(pieces)]

    loads[1].wait()
    loads[2].wait()
    for j, (u, v) in enumerate(zip(rows_of(search_dual, 0), rows_of(search_incr, 0))):
        own_s[:, pl.ds(j * LANES, LANES)] = u
        g_own[0, :, pl.ds(j * LANES, LANES)] = v
        g_own[1, :, pl.ds(j * LANES, LANES)] = u

    ways = (1, -2)
    for k, way in enumerate(ways):
        go(remote(own_s, near_s.at[k], s_send.at[k], s_recv.at[k], at(way)))
        both = pl.ds(2 * k, 2)
        go(remote(w_out.at[both], w_in.at[both, mine], w_send.at[k], w_recv.at[k], at(way)))

    loads[4].wait()
    for c in range(5):
        for j, value in enumerate(rows_of(coefs, c * flat)):
            g_own[2 + c, :, pl.ds(j * LANES, LANES)] = value
    lane = lax.broadcasted_iota(jnp.int32, (levels, LANES), 1)
    lead = g_own[0, :, pl.ds(0, LANES)]
    last = pltpu.roll(g_own[0, :, pl.ds(block - LANES, LANES)], 2, 1)
    for k in range(1, 7):
        chosen = lane // 2 == k
        lead = jnp.where(chosen, pltpu.roll(g_own[k, :, pl.ds(0, LANES)], 2 * k, 1), lead)
        last = jnp.where(chosen, pltpu.roll(g_own[k, :, pl.ds(block - LANES, LANES)], 2 * k + 2, 1), last)
    g_edge[0] = last
    g_edge[1] = lead

    go(remote(g_own, g_lat, g_send.at[0], g_recv.at[0], at(0, True)))

    def edge(side, other):
        n = 1 + 2 * side + other
        way = 1 - 2 * side
        return remote(g_edge.at[side], g_side.at[side, other], g_send.at[n], g_recv.at[n], at(way, other == 1))

    for side in range(2):
        for other in range(2):
            go(edge(side, other))

    for copy in loads[5:]:
        copy.wait()
    resid_sq = jnp.sum(resid_dual[...] ** 2 + resid_obs[...] ** 2 + resid_incr[...] ** 2)
    search_sq = jnp.sum(search_dual[...] ** 2 + search_obs[...] ** 2 + search_incr[...] ** 2)
    first_row = lax.broadcasted_iota(jnp.int32, (8, LANES), 0) == 0
    part[...] = jnp.where(first_row, resid_sq, search_sq)
    part_lon[lon] = part[...]
    for step in range(1, bands):
        go(remote(part, part_lon.at[lon], a_send.at[step], a_recv.at[lon], at(step)))

    for d, step in enumerate((0, -1, 2)):
        slot, found = slot_of(step)
        w_home[d] = jnp.where(found, vals[slot], jnp.zeros((block, block), BF16))
    acc[...] = jnp.zeros_like(acc)

    every = pl.ds(0, WEIGHTS)
    for k in range(2):
        both = pl.ds(2 * k, 2)
        remote(w_out.at[both], w_in.at[both, mine], w_send.at[k], w_recv.at[k], at(0)).wait_recv()
    spot = w_in.at[every, mine]
    for step in range(1, wins):
        go(remote(spot, spot, f_send.at[step], f_recv.at[win], at(0, False, step)))
    lax.fori_loop(0, EARLY, relayed, 0)
    lax.fori_loop(EARLY, 2 * EARLY, first_sends, 0)

    remote(g_own, g_lat, g_send.at[0], g_recv.at[0], at(0)).wait_recv()
    for side in range(2):
        for other in range(2):
            edge(side, other).wait_recv()

    def wide(k, other):
        middle = g_lat if other else g_own
        before = pltpu.roll(g_side[0, other], LANES - 2 - 2 * k, 1)
        after = pltpu.roll(g_side[1, other], (LANES - 2 * k) % LANES, 1)
        return jnp.concatenate([before, middle[k], after], axis=1)

    span = block + 2 * LANES

    def east(x):
        return pltpu.roll(x, span - 1, 1)

    def west(x):
        return pltpu.roll(x, 1, 1)

    here = [wide(k, 0) for k in range(7)]
    over = [wide(k, 1) for k in range(7)]
    south_row = lat == 0
    cross = jnp.where(south_row, here[5], here[6])
    cross_over = jnp.where(south_row, over[6], over[5])

    def forward(v, beyond, c, between):
        return (0.5 + c[2]) * v + c[3] * east(v) + c[4] * west(v) + between * beyond

    def adjoint(u, beyond, c, between):
        return (0.5 + c[2]) * u + west(c[3] * u) + east(c[4] * u) + between * beyond

    once = forward(here[0], over[0], here, cross)
    once_over = forward(over[0], here[0], over, cross_over)
    twice = forward(once, once_over, here, cross)
    back_once = adjoint(here[1], over[1], here, cross_over)
    back_over = adjoint(over[1], here[1], over, cross)
    back_twice = adjoint(back_once, back_over, here, cross_over)
    for j in range(pieces):
        cut = slice((j + 1) * LANES, (j + 2) * LANES)
        moved[0, pl.ds(j, levels, stride=pieces), :] = twice[:, cut]
        moved[1, pl.ds(j, levels, stride=pieces), :] = back_twice[:, cut]
    for k, way in enumerate((1, -1)):
        go(remote(moved.at[k], moved_in.at[k], m_send.at[k], m_recv.at[k], at(0, False, way)))

    for step in range(1, bands):
        source = lax.rem(lon + step, bands)
        remote(part, part_lon.at[source], a_send.at[step], a_recv.at[source], at(0)).wait_recv()
    pair[...] = jnp.sum(part_lon[...], axis=0)
    part_col[color] = pair[...]
    for step in range(1, colors):
        _, where = peer(step)
        go(remote(pair, part_col.at[color], b_send.at[step], b_recv.at[color], where))

    for step in range(1, wins):
        source = lax.rem(win + step, wins)
        remote(spot, spot, f_send.at[step], f_recv.at[source], at(0)).wait_recv()

    def over_lat(w, holder):
        theirs = pl.ds(pl.multiple_of((w * lats + holder) * share, share), share)
        place = w_in.at[every, theirs]
        return remote(place, place, h_send.at[w], h_recv.at[w], at(0, True))

    for w in range(wins):
        go(over_lat(w, lat))
    for k in range(2):
        remote(own_s, near_s.at[k], s_send.at[k], s_recv.at[k], at(0)).wait_recv()

    def spread_of(t):
        def read(ref, search):
            member = ref[...].astype(F32).reshape(group, levels, block)
            product = (member * search[None]).astype(BF16).reshape(rows, block)
            return member, product

        def weigh(member, terms):
            total = sum(jnp.dot(p, w, preferred_element_type=F32) for p, w in terms)
            return jnp.sum(member * total.reshape(group, levels, block), axis=0)

        member, product = read(ens.at[lines(t)], own_s[...])
        first, first_product = read(near.at[0, lines(t)], near_s[0])
        second, second_product = read(near.at[1, lines(t)], near_s[1])
        acc[0] += weigh(member, ((product, w_home[0]), (first_product, w_home[1]), (second_product, w_home[2])))
        acc[1] += weigh(first, ((product, w_in[0]), (second_product, w_in[1])))
        acc[2] += weigh(second, ((product, w_in[2]), (first_product, w_in[3])))

    def step_of(t, carry):
        @pl.when(jnp.logical_and(t >= EARLY, t < CHUNKS))
        def _():
            relayed(t, 0)

        @pl.when(t + 2 * EARLY < CHUNKS)
        def _():
            first_sends(t + 2 * EARLY, 0)

        @pl.when(t == LAG)
        def _():
            for w in range(wins):
                over_lat(w, 1 - lat).wait_recv()

        @pl.when(t >= LAG)
        def _():
            to_west(t - LAG).wait_recv()
            to_east(t - LAG).wait_recv()
            spread_of(t - LAG)

        return carry

    lax.fori_loop(0, CHUNKS + LAG, step_of, 0)

    for k, way in enumerate(ways):
        go(remote(acc.at[1 + k], back.at[k], r_send.at[k], r_recv.at[k], at(-way)))

    for step in range(1, colors):
        source, where = peer(step)
        remote(pair, part_col.at[source], b_send.at[step], b_recv.at[source], where).wait_recv()
    sums = jnp.sum(part_col[...], axis=0)
    alpha = sums[0:1, :] / (sums[1:2, :] + 1e-6)

    out[0] = dual_state[...] + alpha * search_dual[...]
    out[1] = dual_obs[...] + alpha * search_obs[...]
    out[2] = increment[...] + alpha * search_incr[...]
    image_obs = obs_var[...] * search_obs[...] + obs_weight[...] * search_incr[...]
    out[4] = resid_obs[...] - alpha * image_obs
    for k in range(2):
        remote(moved.at[k], moved_in.at[k], m_send.at[k], m_recv.at[k], at(0)).wait_recv()
    later = jnp.where(win < wins - 1, moved_in[1], 0.0)
    image_incr = search_dual[...] - later + obs_weight[...] * search_obs[...]
    out[5] = resid_incr[...] - alpha * image_incr
    prior = jnp.where(win > 0, moved_in[0], 0.0)

    for k in range(2):
        remote(acc.at[1 + k], back.at[k], r_send.at[k], r_recv.at[k], at(0)).wait_recv()
    covar = (acc[0] + back[0] + back[1]) / (members - 1)
    for j in range(pieces):
        covar_flat[pl.ds(j, levels, stride=pieces), :] = covar[:, j * LANES:(j + 1) * LANES]
    image_dual = covar_flat[...] + search_incr[...] - prior
    out[3] = resid_dual[...] - alpha * image_dual

    for copy in started:
        copy.wait_send()

    def sent(t, carry):
        to_west(t).wait_send()
        to_east(t).wait_send()

        @pl.when(lax.rem(t, 2) == parity)
        def _():
            from_relay(t).wait_send()

        return carry

    lax.fori_loop(0, CHUNKS, sent, 0)


def local(wins, bands, lats, *args):
    fields = list(args)
    _, members, levels, _, block = args[9].shape
    flat = levels * block // LANES
    for k in (0, 1, 2, 3, 4, 5, 6, 7, 8, 11, 12):
        fields[k] = args[k].reshape(flat, LANES)
    fields[9] = args[9].reshape(members * levels, block)
    fields[10] = args[10].reshape(5 * flat, LANES)
    fields[14] = args[14][0]
    colors = wins * lats
    share = block // colors
    total = members * levels
    vmem = pl.BlockSpec(memory_space=pltpu.VMEM)
    specs = [pl.BlockSpec(memory_space=pl.ANY)] * 15
    specs[13] = pl.BlockSpec(memory_space=pltpu.SMEM)
    dma = pltpu.SemaphoreType.DMA
    pairs = [(3, CHUNKS), (2,), (2,), (wins,), (wins,), (5,), (bands,), (colors,), (2,), (2,)]
    out = pl.pallas_call(
        functools.partial(kernel, (wins, bands, lats, members, levels, block)),
        out_shape=jax.ShapeDtypeStruct((6, flat, LANES), F32),
        in_specs=specs,
        out_specs=vmem,
        scratch_shapes=[
            pltpu.VMEM(fields[k].shape, fields[k].dtype) for k in range(15) if k != 13
        ] + [
            dma((14,)),
            pltpu.VMEM((2, total, block), BF16),
            pltpu.VMEM((total // 2, block), BF16),
            pltpu.VMEM((2, levels, block), F32),
            pltpu.VMEM((levels, block), F32),
            pltpu.VMEM((3, block, block), BF16),
            pltpu.VMEM((WEIGHTS, share, block), BF16),
            pltpu.VMEM((WEIGHTS, block, block), BF16),
            pltpu.VMEM((7, levels, block), F32),
            pltpu.VMEM((7, levels, block), F32),
            pltpu.VMEM((2, levels, LANES), F32),
            pltpu.VMEM((2, 2, levels, LANES), F32),
            pltpu.VMEM((8, LANES), F32),
            pltpu.VMEM((bands, 8, LANES), F32),
            pltpu.VMEM((8, LANES), F32),
            pltpu.VMEM((colors, 8, LANES), F32),
            pltpu.VMEM((2, flat, LANES), F32),
            pltpu.VMEM((2, flat, LANES), F32),
            pltpu.VMEM((3, levels, block), F32),
            pltpu.VMEM((2, levels, block), F32),
            pltpu.VMEM((flat, LANES), F32),
        ] + [dma(shape) for shape in pairs for _ in range(2)],
        compiler_params=pltpu.CompilerParams(
            collective_id=0, has_side_effects=True, vmem_limit_bytes=60 * 1024 * 1024
        ),
    )(*fields)
    return tuple(out[k].reshape(args[0].shape) for k in range(6))


def solution(mesh):
    wins, bands, lats = (mesh.shape[name] for name in ("win", "lon", "lat"))
    field = P("win", None, "lat", "lon")
    deep = P("win", None, None, "lat", "lon")
    return jax.shard_map(
        functools.partial(local, wins, bands, lats),
        mesh=mesh,
        in_specs=(field,) * 9 + (deep, deep, field, field, P("lon", None), P("lon", None, None, None)),
        out_specs=(field,) * 6,
        check_vma=False,
    )
```

```python
import functools

import jax
import jax.numpy as jnp
from jax import lax
from jax.experimental import pallas as pl
from jax.experimental.pallas import tpu as pltpu
from jax.sharding import PartitionSpec as P

CHUNKS = 8
EARLY = 2
WEIGHTS = 4
LAG = 3
LANES = 128
MESH = pl.DeviceIdType.MESH
BF16 = jnp.bfloat16
F32 = jnp.float32


def remote(src, dst, send, recv, where):
    return pltpu.make_async_remote_copy(
        src_ref=src,
        dst_ref=dst,
        send_sem=send,
        recv_sem=recv,
        device_id=where,
        device_id_type=MESH,
    )


def kernel(
    sizes,
    dual_state_h, dual_obs_h, increment_h,
    resid_dual_h, resid_obs_h, resid_incr_h,
    search_dual_h, search_obs_h, search_incr_h,
    ens_h, coefs_h, obs_weight_h, obs_var_h, cols, vals_h,
    out,
    dual_state, dual_obs, increment,
    resid_dual, resid_obs, resid_incr,
    search_dual, search_obs, search_incr,
    ens, coefs, obs_weight, obs_var, vals, load,
    near, hold, near_s, own_s, w_home, w_out, w_in,
    g_own, g_lat, g_edge, g_side,
    part, part_lon, pair, part_col,
    moved, moved_in, acc, back, covar_flat,
    e_send, e_recv, s_send, s_recv, w_send, w_recv, f_send, f_recv, h_send, h_recv,
    g_send, g_recv, a_send, a_recv, b_send, b_recv,
    m_send, m_recv, r_send, r_recv,
):
    wins, bands, lats, members, levels, block = sizes
    colors = wins * lats
    pieces = block // LANES
    flat = levels * pieces
    rows = members * levels // CHUNKS
    group = rows // levels
    share = block // colors
    win = lax.axis_index("win")
    lon = lax.axis_index("lon")
    lat = lax.axis_index("lat")
    color = win * lats + lat

    def at(lon_step=0, other_lat=False, win_step=0):
        return {
            "win": lax.rem(win + win_step + wins, wins),
            "lon": lax.rem(lon + lon_step + bands, bands),
            "lat": 1 - lat if other_lat else lat,
        }

    def peer(step):
        index = lax.rem(color + step, colors)
        return index, {"win": index // lats, "lon": lon, "lat": lax.rem(index, lats)}

    barrier = pltpu.get_barrier_semaphore()
    greeted = [at(step) for step in range(1, bands)]
    greeted += [peer(step)[1] for step in range(1, colors)]
    greeted += [at(1, True), at(-1, True)]
    for where in greeted:
        pl.semaphore_signal(barrier, inc=1, device_id=where, device_id_type=MESH)

    loads = [
        pltpu.make_async_copy(source, target, load.at[k])
        for k, (source, target) in enumerate((
            (vals_h, vals), (search_dual_h, search_dual), (search_incr_h, search_incr),
            (ens_h, ens), (coefs_h, coefs), (search_obs_h, search_obs),
            (resid_dual_h, resid_dual), (resid_obs_h, resid_obs), (resid_incr_h, resid_incr),
            (dual_state_h, dual_state), (dual_obs_h, dual_obs), (increment_h, increment),
            (obs_weight_h, obs_weight), (obs_var_h, obs_var),
        ))
    ]
    for copy in loads:
        copy.start()

    started = []

    def go(copy):
        copy.start()
        started.append(copy)

    parity = lax.rem(lon, 2)
    even = parity == 0

    def lines(t):
        return pl.ds(pl.multiple_of(t * rows, rows), rows)

    def halves(t):
        return pl.ds(pl.multiple_of(t // 2 * rows, rows), rows)

    def to_west(t):
        return remote(ens.at[lines(t)], near.at[1, lines(t)], e_send.at[0, t], e_recv.at[0, t], at(-2))

    def to_east(t):
        return remote(ens.at[lines(t)], near.at[0, lines(t)], e_send.at[1, t], e_recv.at[1, t], at(1))

    def by_relay(t):
        return lax.rem(t, 2) == 1

    def to_relay(t):
        way = 2
        return remote(ens.at[lines(t)], hold.at[halves(t)], e_send.at[1, t], e_recv.at[2, t], at(way))

    def from_relay(t):
        return remote(hold.at[halves(t)], near.at[0, lines(t)], e_send.at[2, t], e_recv.at[1, t], at(-1))

    def first_sends(t, carry):
        direct_first = lat == 0

        @pl.when(direct_first)
        def _():
            to_west(t).start()

        relay = jnp.logical_and(jnp.logical_not(even), by_relay(t))

        @pl.when(jnp.logical_not(relay))
        def _():
            to_east(t).start()

        @pl.when(relay)
        def _():
            to_relay(t).start()

        @pl.when(jnp.logical_not(direct_first))
        def _():
            to_west(t).start()

        return carry

    def relayed(t, carry):
        @pl.when(jnp.logical_and(parity == 1, by_relay(t)))
        def _():
            to_relay(t).wait_recv()
            from_relay(t).start()

        return carry

    def slot_of(step):
        target = lax.rem(lon + step + bands, bands)
        slot = jnp.int32(0)
        found = jnp.int32(0)
        for j in range(vals.shape[0]):
            hit = cols[0, j] == target
            slot = jnp.where(hit, j, slot)
            found = jnp.where(hit, 1, found)
        return slot, found > 0

    mine = pl.ds(pl.multiple_of(color * share, share), share)
    loads[0].wait()
    for k, step in enumerate((1, 3, -2, -3)):
        slot, found = slot_of(step)
        w_out[k] = jnp.where(found, vals[slot, mine, :], jnp.zeros((share, block), BF16))

    def rows_of(ref, base):
        return [ref[pl.ds(base + j, levels, stride=pieces), :] for j in range(pieces)]

    loads[1].wait()
    loads[2].wait()
    for j, (u, v) in enumerate(zip(rows_of(search_dual, 0), rows_of(search_incr, 0))):
        own_s[:, pl.ds(j * LANES, LANES)] = u
        g_own[0, :, pl.ds(j * LANES, LANES)] = v
        g_own[1, :, pl.ds(j * LANES, LANES)] = u

    loads[3].wait()
    pl.semaphore_wait(barrier, len(greeted))

    ways = (1, -2)
    for k, way in enumerate(ways):
        go(remote(own_s, near_s.at[k], s_send.at[k], s_recv.at[k], at(way)))
        both = pl.ds(2 * k, 2)
        go(remote(w_out.at[both], w_in.at[both, mine], w_send.at[k], w_recv.at[k], at(way)))

    lax.fori_loop(0, EARLY, first_sends, 0)

    loads[4].wait()
    for c in range(5):
        for j, value in enumerate(rows_of(coefs, c * flat)):
            g_own[2 + c, :, pl.ds(j * LANES, LANES)] = value
    lane = lax.broadcasted_iota(jnp.int32, (levels, LANES), 1)
    lead = g_own[0, :, pl.ds(0, LANES)]
    last = pltpu.roll(g_own[0, :, pl.ds(block - LANES, LANES)], 2, 1)
    for k in range(1, 7):
        chosen = lane // 2 == k
        lead = jnp.where(chosen, pltpu.roll(g_own[k, :, pl.ds(0, LANES)], 2 * k, 1), lead)
        last = jnp.where(chosen, pltpu.roll(g_own[k, :, pl.ds(block - LANES, LANES)], 2 * k + 2, 1), last)
    g_edge[0] = last
    g_edge[1] = lead

    go(remote(g_own, g_lat, g_send.at[0], g_recv.at[0], at(0, True)))

    def edge(side, other):
        n = 1 + 2 * side + other
        way = 1 - 2 * side
        return remote(g_edge.at[side], g_side.at[side, other], g_send.at[n], g_recv.at[n], at(way, other == 1))

    for side in range(2):
        for other in range(2):
            go(edge(side, other))

    for copy in loads[5:]:
        copy.wait()
    resid_sq = jnp.sum(resid_dual[...] ** 2 + resid_obs[...] ** 2 + resid_incr[...] ** 2)
    search_sq = jnp.sum(search_dual[...] ** 2 + search_obs[...] ** 2 + search_incr[...] ** 2)
    first_row = lax.broadcasted_iota(jnp.int32, (8, LANES), 0) == 0
    part[...] = jnp.where(first_row, resid_sq, search_sq)
    part_lon[lon] = part[...]
    for step in range(1, bands):
        go(remote(part, part_lon.at[lon], a_send.at[step], a_recv.at[lon], at(step)))

    for d, step in enumerate((0, -1, 2)):
        slot, found = slot_of(step)
        w_home[d] = jnp.where(found, vals[slot], jnp.zeros((block, block), BF16))
    acc[...] = jnp.zeros_like(acc)

    every = pl.ds(0, WEIGHTS)
    for k in range(2):
        both = pl.ds(2 * k, 2)
        remote(w_out.at[both], w_in.at[both, mine], w_send.at[k], w_recv.at[k], at(0)).wait_recv()
    spot = w_in.at[every, mine]
    for step in range(1, wins):
        go(remote(spot, spot, f_send.at[step], f_recv.at[win], at(0, False, step)))
    lax.fori_loop(0, EARLY, relayed, 0)
    lax.fori_loop(EARLY, 2 * EARLY, first_sends, 0)

    remote(g_own, g_lat, g_send.at[0], g_recv.at[0], at(0)).wait_recv()
    for side in range(2):
        for other in range(2):
            edge(side, other).wait_recv()

    def wide(k, other):
        middle = g_lat if other else g_own
        before = pltpu.roll(g_side[0, other], LANES - 2 - 2 * k, 1)
        after = pltpu.roll(g_side[1, other], (LANES - 2 * k) % LANES, 1)
        return jnp.concatenate([before, middle[k], after], axis=1)

    span = block + 2 * LANES

    def east(x):
        return pltpu.roll(x, span - 1, 1)

    def west(x):
        return pltpu.roll(x, 1, 1)

    here = [wide(k, 0) for k in range(7)]
    over = [wide(k, 1) for k in range(7)]
    south_row = lat == 0
    cross = jnp.where(south_row, here[5], here[6])
    cross_over = jnp.where(south_row, over[6], over[5])

    def forward(v, beyond, c, between):
        return (0.5 + c[2]) * v + c[3] * east(v) + c[4] * west(v) + between * beyond

    def adjoint(u, beyond, c, between):
        return (0.5 + c[2]) * u + west(c[3] * u) + east(c[4] * u) + between * beyond

    once = forward(here[0], over[0], here, cross)
    once_over = forward(over[0], here[0], over, cross_over)
    twice = forward(once, once_over, here, cross)
    back_once = adjoint(here[1], over[1], here, cross_over)
    back_over = adjoint(over[1], here[1], over, cross)
    back_twice = adjoint(back_once, back_over, here, cross_over)
    for j in range(pieces):
        cut = slice((j + 1) * LANES, (j + 2) * LANES)
        moved[0, pl.ds(j, levels, stride=pieces), :] = twice[:, cut]
        moved[1, pl.ds(j, levels, stride=pieces), :] = back_twice[:, cut]
    for k, way in enumerate((1, -1)):
        go(remote(moved.at[k], moved_in.at[k], m_send.at[k], m_recv.at[k], at(0, False, way)))

    for step in range(1, bands):
        source = lax.rem(lon + step, bands)
        remote(part, part_lon.at[source], a_send.at[step], a_recv.at[source], at(0)).wait_recv()
    pair[...] = jnp.sum(part_lon[...], axis=0)
    part_col[color] = pair[...]
    for step in range(1, colors):
        _, where = peer(step)
        go(remote(pair, part_col.at[color], b_send.at[step], b_recv.at[color], where))

    for step in range(1, wins):
        source = lax.rem(win + step, wins)
        remote(spot, spot, f_send.at[step], f_recv.at[source], at(0)).wait_recv()

    def over_lat(w, holder):
        theirs = pl.ds(pl.multiple_of((w * lats + holder) * share, share), share)
        place = w_in.at[every, theirs]
        return remote(place, place, h_send.at[w], h_recv.at[w], at(0, True))

    for w in range(wins):
        go(over_lat(w, lat))
    lax.fori_loop(2 * EARLY, CHUNKS, first_sends, 0)
    for k in range(2):
        remote(own_s, near_s.at[k], s_send.at[k], s_recv.at[k], at(0)).wait_recv()

    def spread_of(t):
        def read(ref, search):
            member = ref[...].astype(F32).reshape(group, levels, block)
            product = (member * search[None]).astype(BF16).reshape(rows, block)
            return member, product

        def weigh(member, terms):
            total = sum(jnp.dot(p, w, preferred_element_type=F32) for p, w in terms)
            return jnp.sum(member * total.reshape(group, levels, block), axis=0)

        member, product = read(ens.at[lines(t)], own_s[...])
        first, first_product = read(near.at[0, lines(t)], near_s[0])
        second, second_product = read(near.at[1, lines(t)], near_s[1])
        acc[0] += weigh(member, ((product, w_home[0]), (first_product, w_home[1]), (second_product, w_home[2])))
        acc[1] += weigh(first, ((product, w_in[0]), (second_product, w_in[1])))
        acc[2] += weigh(second, ((product, w_in[2]), (first_product, w_in[3])))

    def step_of(t, carry):
        @pl.when(jnp.logical_and(t >= EARLY, t < CHUNKS))
        def _():
            relayed(t, 0)

        @pl.when(t == LAG)
        def _():
            for w in range(wins):
                over_lat(w, 1 - lat).wait_recv()

        @pl.when(t >= LAG)
        def _():
            to_west(t - LAG).wait_recv()
            to_east(t - LAG).wait_recv()
            spread_of(t - LAG)

        return carry

    lax.fori_loop(0, CHUNKS + LAG, step_of, 0)

    for k, way in enumerate(ways):
        go(remote(acc.at[1 + k], back.at[k], r_send.at[k], r_recv.at[k], at(-way)))

    for step in range(1, colors):
        source, where = peer(step)
        remote(pair, part_col.at[source], b_send.at[step], b_recv.at[source], where).wait_recv()
    sums = jnp.sum(part_col[...], axis=0)
    alpha = sums[0:1, :] / (sums[1:2, :] + 1e-6)

    out[0] = dual_state[...] + alpha * search_dual[...]
    out[1] = dual_obs[...] + alpha * search_obs[...]
    out[2] = increment[...] + alpha * search_incr[...]
    image_obs = obs_var[...] * search_obs[...] + obs_weight[...] * search_incr[...]
    out[4] = resid_obs[...] - alpha * image_obs
    for k in range(2):
        remote(moved.at[k], moved_in.at[k], m_send.at[k], m_recv.at[k], at(0)).wait_recv()
    later = jnp.where(win < wins - 1, moved_in[1], 0.0)
    image_incr = search_dual[...] - later + obs_weight[...] * search_obs[...]
    out[5] = resid_incr[...] - alpha * image_incr
    prior = jnp.where(win > 0, moved_in[0], 0.0)

    for k in range(2):
        remote(acc.at[1 + k], back.at[k], r_send.at[k], r_recv.at[k], at(0)).wait_recv()
    covar = (acc[0] + back[0] + back[1]) / (members - 1)
    for j in range(pieces):
        covar_flat[pl.ds(j, levels, stride=pieces), :] = covar[:, j * LANES:(j + 1) * LANES]
    image_dual = covar_flat[...] + search_incr[...] - prior
    out[3] = resid_dual[...] - alpha * image_dual

    for copy in started:
        copy.wait_send()

    def sent(t, carry):
        to_west(t).wait_send()
        to_east(t).wait_send()

        @pl.when(jnp.logical_and(parity == 1, by_relay(t)))
        def _():
            from_relay(t).wait_send()

        return carry

    lax.fori_loop(0, CHUNKS, sent, 0)


def local(wins, bands, lats, *args):
    fields = list(args)
    _, members, levels, _, block = args[9].shape
    flat = levels * block // LANES
    for k in (0, 1, 2, 3, 4, 5, 6, 7, 8, 11, 12):
        fields[k] = args[k].reshape(flat, LANES)
    fields[9] = args[9].reshape(members * levels, block)
    fields[10] = args[10].reshape(5 * flat, LANES)
    fields[14] = args[14][0]
    colors = wins * lats
    share = block // colors
    total = members * levels
    vmem = pl.BlockSpec(memory_space=pltpu.VMEM)
    specs = [pl.BlockSpec(memory_space=pl.ANY)] * 15
    specs[13] = pl.BlockSpec(memory_space=pltpu.SMEM)
    dma = pltpu.SemaphoreType.DMA
    pairs = [(3, CHUNKS), (2,), (2,), (wins,), (wins,), (5,), (bands,), (colors,), (2,), (2,)]
    out = pl.pallas_call(
        functools.partial(kernel, (wins, bands, lats, members, levels, block)),
        out_shape=jax.ShapeDtypeStruct((6, flat, LANES), F32),
        in_specs=specs,
        out_specs=vmem,
        scratch_shapes=[
            pltpu.VMEM(fields[k].shape, fields[k].dtype) for k in range(15) if k != 13
        ] + [
            dma((14,)),
            pltpu.VMEM((2, total, block), BF16),
            pltpu.VMEM((total // 2, block), BF16),
            pltpu.VMEM((2, levels, block), F32),
            pltpu.VMEM((levels, block), F32),
            pltpu.VMEM((3, block, block), BF16),
            pltpu.VMEM((WEIGHTS, share, block), BF16),
            pltpu.VMEM((WEIGHTS, block, block), BF16),
            pltpu.VMEM((7, levels, block), F32),
            pltpu.VMEM((7, levels, block), F32),
            pltpu.VMEM((2, levels, LANES), F32),
            pltpu.VMEM((2, 2, levels, LANES), F32),
            pltpu.VMEM((8, LANES), F32),
            pltpu.VMEM((bands, 8, LANES), F32),
            pltpu.VMEM((8, LANES), F32),
            pltpu.VMEM((colors, 8, LANES), F32),
            pltpu.VMEM((2, flat, LANES), F32),
            pltpu.VMEM((2, flat, LANES), F32),
            pltpu.VMEM((3, levels, block), F32),
            pltpu.VMEM((2, levels, block), F32),
            pltpu.VMEM((flat, LANES), F32),
        ] + [dma(shape) for shape in pairs for _ in range(2)],
        compiler_params=pltpu.CompilerParams(
            collective_id=0, has_side_effects=True, vmem_limit_bytes=60 * 1024 * 1024
        ),
    )(*fields)
    return tuple(out[k].reshape(args[0].shape) for k in range(6))


def solution(mesh):
    wins, bands, lats = (mesh.shape[name] for name in ("win", "lon", "lat"))
    field = P("win", None, "lat", "lon")
    deep = P("win", None, None, "lat", "lon")
    return jax.shard_map(
        functools.partial(local, wins, bands, lats),
        mesh=mesh,
        in_specs=(field,) * 9 + (deep, deep, field, field, P("lon", None), P("lon", None, None, None)),
        out_specs=(field,) * 6,
        check_vma=False,
    )
```

```python
import functools

import jax
import jax.numpy as jnp
from jax import lax
from jax.experimental import pallas as pl
from jax.experimental.pallas import tpu as pltpu
from jax.sharding import PartitionSpec as P

CHUNKS = 8
EARLY = 2
WEIGHTS = 4
LAG = 4
LANES = 128
MESH = pl.DeviceIdType.MESH
BF16 = jnp.bfloat16
F32 = jnp.float32


def remote(src, dst, send, recv, where):
    return pltpu.make_async_remote_copy(
        src_ref=src,
        dst_ref=dst,
        send_sem=send,
        recv_sem=recv,
        device_id=where,
        device_id_type=MESH,
    )


def kernel(
    sizes,
    dual_state_h, dual_obs_h, increment_h,
    resid_dual_h, resid_obs_h, resid_incr_h,
    search_dual_h, search_obs_h, search_incr_h,
    ens_h, coefs_h, obs_weight_h, obs_var_h, cols, vals_h,
    out,
    dual_state, dual_obs, increment,
    resid_dual, resid_obs, resid_incr,
    search_dual, search_obs, search_incr,
    ens, coefs, obs_weight, obs_var, vals, load,
    near, hold, near_s, own_s, w_home, w_out, w_in,
    g_own, g_lat, g_edge, g_side,
    part, part_lon, pair, part_col,
    moved, moved_in, acc, back, covar_flat,
    e_send, e_recv, s_send, s_recv, w_send, w_recv, f_send, f_recv, h_send, h_recv,
    g_send, g_recv, a_send, a_recv, b_send, b_recv,
    m_send, m_recv, r_send, r_recv,
):
    wins, bands, lats, members, levels, block = sizes
    colors = wins * lats
    pieces = block // LANES
    flat = levels * pieces
    rows = members * levels // CHUNKS
    group = rows // levels
    share = block // colors
    win = lax.axis_index("win")
    lon = lax.axis_index("lon")
    lat = lax.axis_index("lat")
    color = win * lats + lat

    def at(lon_step=0, other_lat=False, win_step=0):
        return {
            "win": lax.rem(win + win_step + wins, wins),
            "lon": lax.rem(lon + lon_step + bands, bands),
            "lat": 1 - lat if other_lat else lat,
        }

    def peer(step):
        index = lax.rem(color + step, colors)
        return index, {"win": index // lats, "lon": lon, "lat": lax.rem(index, lats)}

    barrier = pltpu.get_barrier_semaphore()
    greeted = [at(step) for step in range(1, bands)]
    greeted += [peer(step)[1] for step in range(1, colors)]
    greeted += [at(1, True), at(-1, True)]
    for where in greeted:
        pl.semaphore_signal(barrier, inc=1, device_id=where, device_id_type=MESH)

    loads = [
        pltpu.make_async_copy(source, target, load.at[k])
        for k, (source, target) in enumerate((
            (ens_h, ens), (search_dual_h, search_dual), (search_incr_h, search_incr),
            (vals_h, vals), (coefs_h, coefs), (search_obs_h, search_obs),
            (resid_dual_h, resid_dual), (resid_obs_h, resid_obs), (resid_incr_h, resid_incr),
            (dual_state_h, dual_state), (dual_obs_h, dual_obs), (increment_h, increment),
            (obs_weight_h, obs_weight), (obs_var_h, obs_var),
        ))
    ]
    for copy in loads:
        copy.start()

    started = []

    def go(copy):
        copy.start()
        started.append(copy)

    parity = lax.rem(lon, 2)
    even = parity == 0

    def lines(t):
        return pl.ds(pl.multiple_of(t * rows, rows), rows)

    def to_west(t):
        return remote(ens.at[lines(t)], near.at[1, lines(t)], e_send.at[0, t], e_recv.at[0, t], at(-2))

    def to_east(t):
        return remote(ens.at[lines(t)], near.at[0, lines(t)], e_send.at[1, t], e_recv.at[1, t], at(1))

    def by_relay(t):
        return jnp.logical_or(t < 3, lax.rem(t, 2) == 0)

    def to_relay(t):
        way = -1
        return remote(ens.at[lines(t)], hold.at[lines(t)], e_send.at[1, t], e_recv.at[2, t], at(way))

    def from_relay(t):
        return remote(hold.at[lines(t)], near.at[0, lines(t)], e_send.at[2, t], e_recv.at[1, t], at(2))

    def first_sends(t, carry):
        direct_first = lat == 0

        @pl.when(direct_first)
        def _():
            to_west(t).start()

        relay = jnp.logical_and(jnp.logical_not(even), by_relay(t))

        @pl.when(jnp.logical_not(relay))
        def _():
            to_east(t).start()

        @pl.when(relay)
        def _():
            to_relay(t).start()

        @pl.when(jnp.logical_not(direct_first))
        def _():
            to_west(t).start()

        return carry

    def relayed(t, carry):
        @pl.when(jnp.logical_and(parity == 0, by_relay(t)))
        def _():
            to_relay(t).wait_recv()
            from_relay(t).start()

        return carry

    loads[0].wait()
    pl.semaphore_wait(barrier, len(greeted))
    lax.fori_loop(0, 1, first_sends, 0)

    def slot_of(step):
        target = lax.rem(lon + step + bands, bands)
        slot = jnp.int32(0)
        found = jnp.int32(0)
        for j in range(vals.shape[0]):
            hit = cols[0, j] == target
            slot = jnp.where(hit, j, slot)
            found = jnp.where(hit, 1, found)
        return slot, found > 0

    mine = pl.ds(pl.multiple_of(color * share, share), share)
    loads[3].wait()
    for k, step in enumerate((1, 3, -2, -3)):
        slot, found = slot_of(step)
        w_out[k] = jnp.where(found, vals[slot, mine, :], jnp.zeros((share, block), BF16))

    def rows_of(ref, base):
        return [ref[pl.ds(base + j, levels, stride=pieces), :] for j in range(pieces)]

    loads[1].wait()
    loads[2].wait()
    for j, (u, v) in enumerate(zip(rows_of(search_dual, 0), rows_of(search_incr, 0))):
        own_s[:, pl.ds(j * LANES, LANES)] = u
        g_own[0, :, pl.ds(j * LANES, LANES)] = v
        g_own[1, :, pl.ds(j * LANES, LANES)] = u

    ways = (1, -2)
    for k, way in enumerate(ways):
        go(remote(own_s, near_s.at[k], s_send.at[k], s_recv.at[k], at(way)))
        both = pl.ds(2 * k, 2)
        go(remote(w_out.at[both], w_in.at[both, mine], w_send.at[k], w_recv.at[k], at(way)))

    lax.fori_loop(1, 2 * EARLY, first_sends, 0)

    loads[4].wait()
    for c in range(5):
        for j, value in enumerate(rows_of(coefs, c * flat)):
            g_own[2 + c, :, pl.ds(j * LANES, LANES)] = value
    lane = lax.broadcasted_iota(jnp.int32, (levels, LANES), 1)
    lead = g_own[0, :, pl.ds(0, LANES)]
    last = pltpu.roll(g_own[0, :, pl.ds(block - LANES, LANES)], 2, 1)
    for k in range(1, 7):
        chosen = lane // 2 == k
        lead = jnp.where(chosen, pltpu.roll(g_own[k, :, pl.ds(0, LANES)], 2 * k, 1), lead)
        last = jnp.where(chosen, pltpu.roll(g_own[k, :, pl.ds(block - LANES, LANES)], 2 * k + 2, 1), last)
    g_edge[0] = last
    g_edge[1] = lead

    go(remote(g_own, g_lat, g_send.at[0], g_recv.at[0], at(0, True)))

    def edge(side, other):
        n = 1 + 2 * side + other
        way = 1 - 2 * side
        return remote(g_edge.at[side], g_side.at[side, other], g_send.at[n], g_recv.at[n], at(way, other == 1))

    for side in range(2):
        for other in range(2):
            go(edge(side, other))

    for copy in loads[5:]:
        copy.wait()
    resid_sq = jnp.sum(resid_dual[...] ** 2 + resid_obs[...] ** 2 + resid_incr[...] ** 2)
    search_sq = jnp.sum(search_dual[...] ** 2 + search_obs[...] ** 2 + search_incr[...] ** 2)
    first_row = lax.broadcasted_iota(jnp.int32, (8, LANES), 0) == 0
    part[...] = jnp.where(first_row, resid_sq, search_sq)
    part_lon[lon] = part[...]
    for step in range(1, bands):
        go(remote(part, part_lon.at[lon], a_send.at[step], a_recv.at[lon], at(step)))

    for d, step in enumerate((0, -1, 2)):
        slot, found = slot_of(step)
        w_home[d] = jnp.where(found, vals[slot], jnp.zeros((block, block), BF16))
    acc[...] = jnp.zeros_like(acc)

    every = pl.ds(0, WEIGHTS)
    for k in range(2):
        both = pl.ds(2 * k, 2)
        remote(w_out.at[both], w_in.at[both, mine], w_send.at[k], w_recv.at[k], at(0)).wait_recv()
    spot = w_in.at[every, mine]
    for step in range(1, wins):
        go(remote(spot, spot, f_send.at[step], f_recv.at[win], at(0, False, step)))
    lax.fori_loop(0, EARLY, relayed, 0)
    lax.fori_loop(2 * EARLY, 3 * EARLY, first_sends, 0)

    remote(g_own, g_lat, g_send.at[0], g_recv.at[0], at(0)).wait_recv()
    for side in range(2):
        for other in range(2):
            edge(side, other).wait_recv()

    def wide(k, other):
        middle = g_lat if other else g_own
        before = pltpu.roll(g_side[0, other], LANES - 2 - 2 * k, 1)
        after = pltpu.roll(g_side[1, other], (LANES - 2 * k) % LANES, 1)
        return jnp.concatenate([before, middle[k], after], axis=1)

    span = block + 2 * LANES

    def east(x):
        return pltpu.roll(x, span - 1, 1)

    def west(x):
        return pltpu.roll(x, 1, 1)

    here = [wide(k, 0) for k in range(7)]
    over = [wide(k, 1) for k in range(7)]
    south_row = lat == 0
    cross = jnp.where(south_row, here[5], here[6])
    cross_over = jnp.where(south_row, over[6], over[5])

    def forward(v, beyond, c, between):
        return (0.5 + c[2]) * v + c[3] * east(v) + c[4] * west(v) + between * beyond

    def adjoint(u, beyond, c, between):
        return (0.5 + c[2]) * u + west(c[3] * u) + east(c[4] * u) + between * beyond

    once = forward(here[0], over[0], here, cross)
    once_over = forward(over[0], here[0], over, cross_over)
    twice = forward(once, once_over, here, cross)
    back_once = adjoint(here[1], over[1], here, cross_over)
    back_over = adjoint(over[1], here[1], over, cross)
    back_twice = adjoint(back_once, back_over, here, cross_over)
    for j in range(pieces):
        cut = slice((j + 1) * LANES, (j + 2) * LANES)
        moved[0, pl.ds(j, levels, stride=pieces), :] = twice[:, cut]
        moved[1, pl.ds(j, levels, stride=pieces), :] = back_twice[:, cut]
    for k, way in enumerate((1, -1)):
        go(remote(moved.at[k], moved_in.at[k], m_send.at[k], m_recv.at[k], at(0, False, way)))

    for step in range(1, bands):
        source = lax.rem(lon + step, bands)
        remote(part, part_lon.at[source], a_send.at[step], a_recv.at[source], at(0)).wait_recv()
    pair[...] = jnp.sum(part_lon[...], axis=0)
    part_col[color] = pair[...]
    for step in range(1, colors):
        _, where = peer(step)
        go(remote(pair, part_col.at[color], b_send.at[step], b_recv.at[color], where))

    for step in range(1, wins):
        source = lax.rem(win + step, wins)
        remote(spot, spot, f_send.at[step], f_recv.at[source], at(0)).wait_recv()

    def over_lat(w, holder):
        theirs = pl.ds(pl.multiple_of((w * lats + holder) * share, share), share)
        place = w_in.at[every, theirs]
        return remote(place, place, h_send.at[w], h_recv.at[w], at(0, True))

    for w in range(wins):
        go(over_lat(w, lat))
    lax.fori_loop(3 * EARLY, CHUNKS, first_sends, 0)
    for k in range(2):
        remote(own_s, near_s.at[k], s_send.at[k], s_recv.at[k], at(0)).wait_recv()

    def spread_of(t):
        def read(ref, search):
            member = ref[...].astype(F32).reshape(group, levels, block)
            product = (member * search[None]).astype(BF16).reshape(rows, block)
            return member, product

        def weigh(member, terms):
            total = sum(jnp.dot(p, w, preferred_element_type=F32) for p, w in terms)
            return jnp.sum(member * total.reshape(group, levels, block), axis=0)

        member, product = read(ens.at[lines(t)], own_s[...])
        first, first_product = read(near.at[0, lines(t)], near_s[0])
        second, second_product = read(near.at[1, lines(t)], near_s[1])
        acc[0] += weigh(member, ((product, w_home[0]), (first_product, w_home[1]), (second_product, w_home[2])))
        acc[1] += weigh(first, ((product, w_in[0]), (second_product, w_in[1])))
        acc[2] += weigh(second, ((product, w_in[2]), (first_product, w_in[3])))

    def step_of(t, carry):
        @pl.when(jnp.logical_and(t >= EARLY, t < CHUNKS))
        def _():
            relayed(t, 0)

        @pl.when(t == LAG)
        def _():
            for w in range(wins):
                over_lat(w, 1 - lat).wait_recv()

        @pl.when(t >= LAG)
        def _():
            to_west(t - LAG).wait_recv()
            to_east(t - LAG).wait_recv()
            spread_of(t - LAG)

        return carry

    lax.fori_loop(0, CHUNKS + LAG, step_of, 0)

    for k, way in enumerate(ways):
        go(remote(acc.at[1 + k], back.at[k], r_send.at[k], r_recv.at[k], at(-way)))

    for step in range(1, colors):
        source, where = peer(step)
        remote(pair, part_col.at[source], b_send.at[step], b_recv.at[source], where).wait_recv()
    sums = jnp.sum(part_col[...], axis=0)
    alpha = sums[0:1, :] / (sums[1:2, :] + 1e-6)

    out[0] = dual_state[...] + alpha * search_dual[...]
    out[1] = dual_obs[...] + alpha * search_obs[...]
    out[2] = increment[...] + alpha * search_incr[...]
    image_obs = obs_var[...] * search_obs[...] + obs_weight[...] * search_incr[...]
    out[4] = resid_obs[...] - alpha * image_obs
    for k in range(2):
        remote(moved.at[k], moved_in.at[k], m_send.at[k], m_recv.at[k], at(0)).wait_recv()
    later = jnp.where(win < wins - 1, moved_in[1], 0.0)
    image_incr = search_dual[...] - later + obs_weight[...] * search_obs[...]
    out[5] = resid_incr[...] - alpha * image_incr
    prior = jnp.where(win > 0, moved_in[0], 0.0)

    for k in range(2):
        remote(acc.at[1 + k], back.at[k], r_send.at[k], r_recv.at[k], at(0)).wait_recv()
    covar = (acc[0] + back[0] + back[1]) / (members - 1)
    for j in range(pieces):
        covar_flat[pl.ds(j, levels, stride=pieces), :] = covar[:, j * LANES:(j + 1) * LANES]
    image_dual = covar_flat[...] + search_incr[...] - prior
    out[3] = resid_dual[...] - alpha * image_dual

    for copy in started:
        copy.wait_send()

    def sent(t, carry):
        to_west(t).wait_send()
        to_east(t).wait_send()

        @pl.when(jnp.logical_and(parity == 0, by_relay(t)))
        def _():
            from_relay(t).wait_send()

        return carry

    lax.fori_loop(0, CHUNKS, sent, 0)


def local(wins, bands, lats, *args):
    fields = list(args)
    _, members, levels, _, block = args[9].shape
    flat = levels * block // LANES
    for k in (0, 1, 2, 3, 4, 5, 6, 7, 8, 11, 12):
        fields[k] = args[k].reshape(flat, LANES)
    fields[9] = args[9].reshape(members * levels, block)
    fields[10] = args[10].reshape(5 * flat, LANES)
    fields[14] = args[14][0]
    colors = wins * lats
    share = block // colors
    total = members * levels
    vmem = pl.BlockSpec(memory_space=pltpu.VMEM)
    specs = [pl.BlockSpec(memory_space=pl.ANY)] * 15
    specs[13] = pl.BlockSpec(memory_space=pltpu.SMEM)
    dma = pltpu.SemaphoreType.DMA
    pairs = [(3, CHUNKS), (2,), (2,), (wins,), (wins,), (5,), (bands,), (colors,), (2,), (2,)]
    out = pl.pallas_call(
        functools.partial(kernel, (wins, bands, lats, members, levels, block)),
        out_shape=jax.ShapeDtypeStruct((6, flat, LANES), F32),
        in_specs=specs,
        out_specs=vmem,
        scratch_shapes=[
            pltpu.VMEM(fields[k].shape, fields[k].dtype) for k in range(15) if k != 13
        ] + [
            dma((14,)),
            pltpu.VMEM((2, total, block), BF16),
            pltpu.VMEM((total, block), BF16),
            pltpu.VMEM((2, levels, block), F32),
            pltpu.VMEM((levels, block), F32),
            pltpu.VMEM((3, block, block), BF16),
            pltpu.VMEM((WEIGHTS, share, block), BF16),
            pltpu.VMEM((WEIGHTS, block, block), BF16),
            pltpu.VMEM((7, levels, block), F32),
            pltpu.VMEM((7, levels, block), F32),
            pltpu.VMEM((2, levels, LANES), F32),
            pltpu.VMEM((2, 2, levels, LANES), F32),
            pltpu.VMEM((8, LANES), F32),
            pltpu.VMEM((bands, 8, LANES), F32),
            pltpu.VMEM((8, LANES), F32),
            pltpu.VMEM((colors, 8, LANES), F32),
            pltpu.VMEM((2, flat, LANES), F32),
            pltpu.VMEM((2, flat, LANES), F32),
            pltpu.VMEM((3, levels, block), F32),
            pltpu.VMEM((2, levels, block), F32),
            pltpu.VMEM((flat, LANES), F32),
        ] + [dma(shape) for shape in pairs for _ in range(2)],
        compiler_params=pltpu.CompilerParams(
            collective_id=0, has_side_effects=True, vmem_limit_bytes=60 * 1024 * 1024
        ),
    )(*fields)
    return tuple(out[k].reshape(args[0].shape) for k in range(6))


def solution(mesh):
    wins, bands, lats = (mesh.shape[name] for name in ("win", "lon", "lat"))
    field = P("win", None, "lat", "lon")
    deep = P("win", None, None, "lat", "lon")
    return jax.shard_map(
        functools.partial(local, wins, bands, lats),
        mesh=mesh,
        in_specs=(field,) * 9 + (deep, deep, field, field, P("lon", None), P("lon", None, None, None)),
        out_specs=(field,) * 6,
        check_vma=False,
    )
```

```python
import functools

import jax
import jax.numpy as jnp
from jax import lax
from jax.experimental import pallas as pl
from jax.experimental.pallas import tpu as pltpu
from jax.sharding import PartitionSpec as P

CHUNKS = 16
EARLY = 4
WEIGHTS = 4
LAG = 6
LANES = 128
MESH = pl.DeviceIdType.MESH
BF16 = jnp.bfloat16
F32 = jnp.float32


def remote(src, dst, send, recv, where):
    return pltpu.make_async_remote_copy(
        src_ref=src,
        dst_ref=dst,
        send_sem=send,
        recv_sem=recv,
        device_id=where,
        device_id_type=MESH,
    )


def kernel(
    sizes,
    dual_state_h, dual_obs_h, increment_h,
    resid_dual_h, resid_obs_h, resid_incr_h,
    search_dual_h, search_obs_h, search_incr_h,
    ens_h, coefs_h, obs_weight_h, obs_var_h, cols, vals_h,
    out,
    dual_state, dual_obs, increment,
    resid_dual, resid_obs, resid_incr,
    search_dual, search_obs, search_incr,
    ens, coefs, obs_weight, obs_var, vals, load,
    near, hold, near_s, own_s, w_home, w_out, w_in,
    g_own, g_lat, g_edge, g_side,
    part, part_lon, pair, part_col,
    moved, moved_in, acc, back, covar_flat,
    e_send, e_recv, s_send, s_recv, w_send, w_recv, f_send, f_recv, h_send, h_recv,
    g_send, g_recv, a_send, a_recv, b_send, b_recv,
    m_send, m_recv, r_send, r_recv,
):
    wins, bands, lats, members, levels, block = sizes
    colors = wins * lats
    pieces = block // LANES
    flat = levels * pieces
    rows = members * levels // CHUNKS
    group = rows // levels
    share = block // colors
    win = lax.axis_index("win")
    lon = lax.axis_index("lon")
    lat = lax.axis_index("lat")
    color = win * lats + lat

    def at(lon_step=0, other_lat=False, win_step=0):
        return {
            "win": lax.rem(win + win_step + wins, wins),
            "lon": lax.rem(lon + lon_step + bands, bands),
            "lat": 1 - lat if other_lat else lat,
        }

    def peer(step):
        index = lax.rem(color + step, colors)
        return index, {"win": index // lats, "lon": lon, "lat": lax.rem(index, lats)}

    barrier = pltpu.get_barrier_semaphore()
    greeted = [at(step) for step in range(1, bands)]
    greeted += [peer(step)[1] for step in range(1, colors)]
    greeted += [at(1, True), at(-1, True)]
    for where in greeted:
        pl.semaphore_signal(barrier, inc=1, device_id=where, device_id_type=MESH)

    loads = [
        pltpu.make_async_copy(source, target, load.at[k])
        for k, (source, target) in enumerate((
            (ens_h, ens), (search_dual_h, search_dual), (search_incr_h, search_incr),
            (vals_h, vals), (coefs_h, coefs), (search_obs_h, search_obs),
            (resid_dual_h, resid_dual), (resid_obs_h, resid_obs), (resid_incr_h, resid_incr),
            (dual_state_h, dual_state), (dual_obs_h, dual_obs), (increment_h, increment),
            (obs_weight_h, obs_weight), (obs_var_h, obs_var),
        ))
    ]
    for copy in loads:
        copy.start()

    started = []

    def go(copy):
        copy.start()
        started.append(copy)

    parity = lax.rem(lon, 2)
    even = parity == 0

    def lines(t):
        return pl.ds(pl.multiple_of(t * rows, rows), rows)

    def to_west(t):
        return remote(ens.at[lines(t)], near.at[1, lines(t)], e_send.at[0, t], e_recv.at[0, t], at(-2))

    def to_east(t):
        return remote(ens.at[lines(t)], near.at[0, lines(t)], e_send.at[1, t], e_recv.at[1, t], at(1))

    def by_relay(t):
        return jnp.logical_or(lax.rem(t, 8) < 3, lax.rem(t, 2) == 0)

    def to_relay(t):
        way = -1
        return remote(ens.at[lines(t)], hold.at[lines(t)], e_send.at[1, t], e_recv.at[2, t], at(way))

    def from_relay(t):
        return remote(hold.at[lines(t)], near.at[0, lines(t)], e_send.at[2, t], e_recv.at[1, t], at(2))

    def first_sends(t, carry):
        direct_first = lat == 0

        @pl.when(direct_first)
        def _():
            to_west(t).start()

        relay = jnp.logical_and(jnp.logical_not(even), by_relay(t))

        @pl.when(jnp.logical_not(relay))
        def _():
            to_east(t).start()

        @pl.when(relay)
        def _():
            to_relay(t).start()

        @pl.when(jnp.logical_not(direct_first))
        def _():
            to_west(t).start()

        return carry

    def relayed(t, carry):
        @pl.when(jnp.logical_and(parity == 0, by_relay(t)))
        def _():
            to_relay(t).wait_recv()
            from_relay(t).start()

        return carry

    loads[0].wait()
    pl.semaphore_wait(barrier, len(greeted))
    lax.fori_loop(0, 2, first_sends, 0)

    def slot_of(step):
        target = lax.rem(lon + step + bands, bands)
        slot = jnp.int32(0)
        found = jnp.int32(0)
        for j in range(vals.shape[0]):
            hit = cols[0, j] == target
            slot = jnp.where(hit, j, slot)
            found = jnp.where(hit, 1, found)
        return slot, found > 0

    mine = pl.ds(pl.multiple_of(color * share, share), share)
    loads[3].wait()
    for k, step in enumerate((1, 3, -2, -3)):
        slot, found = slot_of(step)
        w_out[k] = jnp.where(found, vals[slot, mine, :], jnp.zeros((share, block), BF16))

    def rows_of(ref, base):
        return [ref[pl.ds(base + j, levels, stride=pieces), :] for j in range(pieces)]

    loads[1].wait()
    loads[2].wait()
    for j, (u, v) in enumerate(zip(rows_of(search_dual, 0), rows_of(search_incr, 0))):
        own_s[:, pl.ds(j * LANES, LANES)] = u
        g_own[0, :, pl.ds(j * LANES, LANES)] = v
        g_own[1, :, pl.ds(j * LANES, LANES)] = u

    ways = (1, -2)
    for k, way in enumerate(ways):
        go(remote(own_s, near_s.at[k], s_send.at[k], s_recv.at[k], at(way)))
        both = pl.ds(2 * k, 2)
        go(remote(w_out.at[both], w_in.at[both, mine], w_send.at[k], w_recv.at[k], at(way)))

    lax.fori_loop(2, 2 * EARLY, first_sends, 0)

    loads[4].wait()
    for c in range(5):
        for j, value in enumerate(rows_of(coefs, c * flat)):
            g_own[2 + c, :, pl.ds(j * LANES, LANES)] = value
    lane = lax.broadcasted_iota(jnp.int32, (levels, LANES), 1)
    lead = g_own[0, :, pl.ds(0, LANES)]
    last = pltpu.roll(g_own[0, :, pl.ds(block - LANES, LANES)], 2, 1)
    for k in range(1, 7):
        chosen = lane // 2 == k
        lead = jnp.where(chosen, pltpu.roll(g_own[k, :, pl.ds(0, LANES)], 2 * k, 1), lead)
        last = jnp.where(chosen, pltpu.roll(g_own[k, :, pl.ds(block - LANES, LANES)], 2 * k + 2, 1), last)
    g_edge[0] = last
    g_edge[1] = lead

    go(remote(g_own, g_lat, g_send.at[0], g_recv.at[0], at(0, True)))

    def edge(side, other):
        n = 1 + 2 * side + other
        way = 1 - 2 * side
        return remote(g_edge.at[side], g_side.at[side, other], g_send.at[n], g_recv.at[n], at(way, other == 1))

    for side in range(2):
        for other in range(2):
            go(edge(side, other))

    for copy in loads[5:]:
        copy.wait()
    resid_sq = jnp.sum(resid_dual[...] ** 2 + resid_obs[...] ** 2 + resid_incr[...] ** 2)
    search_sq = jnp.sum(search_dual[...] ** 2 + search_obs[...] ** 2 + search_incr[...] ** 2)
    first_row = lax.broadcasted_iota(jnp.int32, (8, LANES), 0) == 0
    part[...] = jnp.where(first_row, resid_sq, search_sq)
    part_lon[lon] = part[...]
    for step in range(1, bands):
        go(remote(part, part_lon.at[lon], a_send.at[step], a_recv.at[lon], at(step)))

    for d, step in enumerate((0, -1, 2)):
        slot, found = slot_of(step)
        w_home[d] = jnp.where(found, vals[slot], jnp.zeros((block, block), BF16))
    acc[...] = jnp.zeros_like(acc)

    every = pl.ds(0, WEIGHTS)
    for k in range(2):
        both = pl.ds(2 * k, 2)
        remote(w_out.at[both], w_in.at[both, mine], w_send.at[k], w_recv.at[k], at(0)).wait_recv()
    spot = w_in.at[every, mine]
    for step in range(1, wins):
        go(remote(spot, spot, f_send.at[step], f_recv.at[win], at(0, False, step)))
    lax.fori_loop(0, EARLY, relayed, 0)
    lax.fori_loop(2 * EARLY, 3 * EARLY, first_sends, 0)

    remote(g_own, g_lat, g_send.at[0], g_recv.at[0], at(0)).wait_recv()
    for side in range(2):
        for other in range(2):
            edge(side, other).wait_recv()

    def wide(k, other):
        middle = g_lat if other else g_own
        before = pltpu.roll(g_side[0, other], LANES - 2 - 2 * k, 1)
        after = pltpu.roll(g_side[1, other], (LANES - 2 * k) % LANES, 1)
        return jnp.concatenate([before, middle[k], after], axis=1)

    span = block + 2 * LANES

    def east(x):
        return pltpu.roll(x, span - 1, 1)

    def west(x):
        return pltpu.roll(x, 1, 1)

    here = [wide(k, 0) for k in range(7)]
    over = [wide(k, 1) for k in range(7)]
    south_row = lat == 0
    cross = jnp.where(south_row, here[5], here[6])
    cross_over = jnp.where(south_row, over[6], over[5])

    def forward(v, beyond, c, between):
        return (0.5 + c[2]) * v + c[3] * east(v) + c[4] * west(v) + between * beyond

    def adjoint(u, beyond, c, between):
        return (0.5 + c[2]) * u + west(c[3] * u) + east(c[4] * u) + between * beyond

    once = forward(here[0], over[0], here, cross)
    once_over = forward(over[0], here[0], over, cross_over)
    twice = forward(once, once_over, here, cross)
    back_once = adjoint(here[1], over[1], here, cross_over)
    back_over = adjoint(over[1], here[1], over, cross)
    back_twice = adjoint(back_once, back_over, here, cross_over)
    for j in range(pieces):
        cut = slice((j + 1) * LANES, (j + 2) * LANES)
        moved[0, pl.ds(j, levels, stride=pieces), :] = twice[:, cut]
        moved[1, pl.ds(j, levels, stride=pieces), :] = back_twice[:, cut]
    for k, way in enumerate((1, -1)):
        go(remote(moved.at[k], moved_in.at[k], m_send.at[k], m_recv.at[k], at(0, False, way)))

    for step in range(1, bands):
        source = lax.rem(lon + step, bands)
        remote(part, part_lon.at[source], a_send.at[step], a_recv.at[source], at(0)).wait_recv()
    pair[...] = jnp.sum(part_lon[...], axis=0)
    part_col[color] = pair[...]
    for step in range(1, colors):
        _, where = peer(step)
        go(remote(pair, part_col.at[color], b_send.at[step], b_recv.at[color], where))

    for step in range(1, wins):
        source = lax.rem(win + step, wins)
        remote(spot, spot, f_send.at[step], f_recv.at[source], at(0)).wait_recv()

    def over_lat(w, holder):
        theirs = pl.ds(pl.multiple_of((w * lats + holder) * share, share), share)
        place = w_in.at[every, theirs]
        return remote(place, place, h_send.at[w], h_recv.at[w], at(0, True))

    for w in range(wins):
        go(over_lat(w, lat))
    lax.fori_loop(3 * EARLY, CHUNKS, first_sends, 0)
    for k in range(2):
        remote(own_s, near_s.at[k], s_send.at[k], s_recv.at[k], at(0)).wait_recv()

    def spread_of(t):
        def read(ref, search):
            member = ref[...].astype(F32).reshape(group, levels, block)
            product = (member * search[None]).astype(BF16).reshape(rows, block)
            return member, product

        def weigh(member, terms):
            total = sum(jnp.dot(p, w, preferred_element_type=F32) for p, w in terms)
            return jnp.sum(member * total.reshape(group, levels, block), axis=0)

        member, product = read(ens.at[lines(t)], own_s[...])
        first, first_product = read(near.at[0, lines(t)], near_s[0])
        second, second_product = read(near.at[1, lines(t)], near_s[1])
        acc[0] += weigh(member, ((product, w_home[0]), (first_product, w_home[1]), (second_product, w_home[2])))
        acc[1] += weigh(first, ((product, w_in[0]), (second_product, w_in[1])))
        acc[2] += weigh(second, ((product, w_in[2]), (first_product, w_in[3])))

    def step_of(t, carry):
        @pl.when(jnp.logical_and(t >= EARLY, t < CHUNKS))
        def _():
            relayed(t, 0)

        @pl.when(t == LAG)
        def _():
            for w in range(wins):
                over_lat(w, 1 - lat).wait_recv()

        @pl.when(t >= LAG)
        def _():
            to_west(t - LAG).wait_recv()
            to_east(t - LAG).wait_recv()
            spread_of(t - LAG)

        return carry

    lax.fori_loop(0, CHUNKS + LAG, step_of, 0)

    for k, way in enumerate(ways):
        go(remote(acc.at[1 + k], back.at[k], r_send.at[k], r_recv.at[k], at(-way)))

    for step in range(1, colors):
        source, where = peer(step)
        remote(pair, part_col.at[source], b_send.at[step], b_recv.at[source], where).wait_recv()
    sums = jnp.sum(part_col[...], axis=0)
    alpha = sums[0:1, :] / (sums[1:2, :] + 1e-6)

    out[0] = dual_state[...] + alpha * search_dual[...]
    out[1] = dual_obs[...] + alpha * search_obs[...]
    out[2] = increment[...] + alpha * search_incr[...]
    image_obs = obs_var[...] * search_obs[...] + obs_weight[...] * search_incr[...]
    out[4] = resid_obs[...] - alpha * image_obs
    for k in range(2):
        remote(moved.at[k], moved_in.at[k], m_send.at[k], m_recv.at[k], at(0)).wait_recv()
    later = jnp.where(win < wins - 1, moved_in[1], 0.0)
    image_incr = search_dual[...] - later + obs_weight[...] * search_obs[...]
    out[5] = resid_incr[...] - alpha * image_incr
    prior = jnp.where(win > 0, moved_in[0], 0.0)

    for k in range(2):
        remote(acc.at[1 + k], back.at[k], r_send.at[k], r_recv.at[k], at(0)).wait_recv()
    covar = (acc[0] + back[0] + back[1]) / (members - 1)
    for j in range(pieces):
        covar_flat[pl.ds(j, levels, stride=pieces), :] = covar[:, j * LANES:(j + 1) * LANES]
    image_dual = covar_flat[...] + search_incr[...] - prior
    out[3] = resid_dual[...] - alpha * image_dual

    for copy in started:
        copy.wait_send()

    def sent(t, carry):
        to_west(t).wait_send()
        to_east(t).wait_send()

        @pl.when(jnp.logical_and(parity == 0, by_relay(t)))
        def _():
            from_relay(t).wait_send()

        return carry

    lax.fori_loop(0, CHUNKS, sent, 0)


def local(wins, bands, lats, *args):
    fields = list(args)
    _, members, levels, _, block = args[9].shape
    flat = levels * block // LANES
    for k in (0, 1, 2, 3, 4, 5, 6, 7, 8, 11, 12):
        fields[k] = args[k].reshape(flat, LANES)
    fields[9] = args[9].reshape(members * levels, block)
    fields[10] = args[10].reshape(5 * flat, LANES)
    fields[14] = args[14][0]
    colors = wins * lats
    share = block // colors
    total = members * levels
    vmem = pl.BlockSpec(memory_space=pltpu.VMEM)
    specs = [pl.BlockSpec(memory_space=pl.ANY)] * 15
    specs[13] = pl.BlockSpec(memory_space=pltpu.SMEM)
    dma = pltpu.SemaphoreType.DMA
    pairs = [(3, CHUNKS), (2,), (2,), (wins,), (wins,), (5,), (bands,), (colors,), (2,), (2,)]
    out = pl.pallas_call(
        functools.partial(kernel, (wins, bands, lats, members, levels, block)),
        out_shape=jax.ShapeDtypeStruct((6, flat, LANES), F32),
        in_specs=specs,
        out_specs=vmem,
        scratch_shapes=[
            pltpu.VMEM(fields[k].shape, fields[k].dtype) for k in range(15) if k != 13
        ] + [
            dma((14,)),
            pltpu.VMEM((2, total, block), BF16),
            pltpu.VMEM((total, block), BF16),
            pltpu.VMEM((2, levels, block), F32),
            pltpu.VMEM((levels, block), F32),
            pltpu.VMEM((3, block, block), BF16),
            pltpu.VMEM((WEIGHTS, share, block), BF16),
            pltpu.VMEM((WEIGHTS, block, block), BF16),
            pltpu.VMEM((7, levels, block), F32),
            pltpu.VMEM((7, levels, block), F32),
            pltpu.VMEM((2, levels, LANES), F32),
            pltpu.VMEM((2, 2, levels, LANES), F32),
            pltpu.VMEM((8, LANES), F32),
            pltpu.VMEM((bands, 8, LANES), F32),
            pltpu.VMEM((8, LANES), F32),
            pltpu.VMEM((colors, 8, LANES), F32),
            pltpu.VMEM((2, flat, LANES), F32),
            pltpu.VMEM((2, flat, LANES), F32),
            pltpu.VMEM((3, levels, block), F32),
            pltpu.VMEM((2, levels, block), F32),
            pltpu.VMEM((flat, LANES), F32),
        ] + [dma(shape) for shape in pairs for _ in range(2)],
        compiler_params=pltpu.CompilerParams(
            collective_id=0, has_side_effects=True, vmem_limit_bytes=60 * 1024 * 1024
        ),
    )(*fields)
    return tuple(out[k].reshape(args[0].shape) for k in range(6))


def solution(mesh):
    wins, bands, lats = (mesh.shape[name] for name in ("win", "lon", "lat"))
    field = P("win", None, "lat", "lon")
    deep = P("win", None, None, "lat", "lon")
    return jax.shard_map(
        functools.partial(local, wins, bands, lats),
        mesh=mesh,
        in_specs=(field,) * 9 + (deep, deep, field, field, P("lon", None), P("lon", None, None, None)),
        out_specs=(field,) * 6,
        check_vma=False,
    )
```

```python
import functools

import jax
import jax.numpy as jnp
from jax import lax
from jax.experimental import pallas as pl
from jax.experimental.pallas import tpu as pltpu
from jax.sharding import PartitionSpec as P

CHUNKS = 8
EARLY = 2
WEIGHTS = 4
LAG = 4
LANES = 128
MESH = pl.DeviceIdType.MESH
BF16 = jnp.bfloat16
F32 = jnp.float32


def remote(src, dst, send, recv, where):
    return pltpu.make_async_remote_copy(
        src_ref=src,
        dst_ref=dst,
        send_sem=send,
        recv_sem=recv,
        device_id=where,
        device_id_type=MESH,
    )


def kernel(
    sizes,
    dual_state_h, dual_obs_h, increment_h,
    resid_dual_h, resid_obs_h, resid_incr_h,
    search_dual_h, search_obs_h, search_incr_h,
    ens_h, coefs_h, obs_weight_h, obs_var_h, cols, vals_h,
    out,
    dual_state, dual_obs, increment,
    resid_dual, resid_obs, resid_incr,
    search_dual, search_obs, search_incr,
    ens, coefs, obs_weight, obs_var, vals, load,
    near, hold, near_s, own_s, w_home, w_out, w_in,
    g_own, g_lat, g_edge, g_side,
    part, part_lon, pair, part_col,
    moved, moved_in, acc, back, covar_flat,
    e_send, e_recv, s_send, s_recv, w_send, w_recv, f_send, f_recv, h_send, h_recv,
    g_send, g_recv, a_send, a_recv, b_send, b_recv,
    m_send, m_recv, r_send, r_recv,
):
    wins, bands, lats, members, levels, block = sizes
    colors = wins * lats
    pieces = block // LANES
    flat = levels * pieces
    rows = members * levels // CHUNKS
    group = rows // levels
    share = block // colors
    win = lax.axis_index("win")
    lon = lax.axis_index("lon")
    lat = lax.axis_index("lat")
    color = win * lats + lat

    def at(lon_step=0, other_lat=False, win_step=0):
        return {
            "win": lax.rem(win + win_step + wins, wins),
            "lon": lax.rem(lon + lon_step + bands, bands),
            "lat": 1 - lat if other_lat else lat,
        }

    def peer(step):
        index = lax.rem(color + step, colors)
        return index, {"win": index // lats, "lon": lon, "lat": lax.rem(index, lats)}

    barrier = pltpu.get_barrier_semaphore()
    greeted = [at(step) for step in range(1, bands)]
    greeted += [peer(step)[1] for step in range(1, colors)]
    greeted += [at(1, True), at(-1, True)]
    for where in greeted:
        pl.semaphore_signal(barrier, inc=1, device_id=where, device_id_type=MESH)

    loads = [
        pltpu.make_async_copy(source, target, load.at[k])
        for k, (source, target) in enumerate((
            (ens_h, ens), (search_dual_h, search_dual), (search_incr_h, search_incr),
            (vals_h, vals), (coefs_h, coefs), (search_obs_h, search_obs),
            (resid_dual_h, resid_dual), (resid_obs_h, resid_obs), (resid_incr_h, resid_incr),
            (dual_state_h, dual_state), (dual_obs_h, dual_obs), (increment_h, increment),
            (obs_weight_h, obs_weight), (obs_var_h, obs_var),
        ))
    ]
    for copy in loads:
        copy.start()

    started = []

    def go(copy):
        copy.start()
        started.append(copy)

    parity = lax.rem(lon, 2)
    even = parity == 0

    def lines(t):
        return pl.ds(pl.multiple_of(t * rows, rows), rows)

    def to_west(t):
        return remote(ens.at[lines(t)], near.at[1, lines(t)], e_send.at[0, t], e_recv.at[0, t], at(-2))

    def to_east(t):
        return remote(ens.at[lines(t)], near.at[0, lines(t)], e_send.at[1, t], e_recv.at[1, t], at(1))

    def by_relay(t):
        return jnp.logical_or(t < 3, lax.rem(t, 2) == 0)

    def to_relay(t):
        way = -1
        return remote(ens.at[lines(t)], hold.at[lines(t)], e_send.at[1, t], e_recv.at[2, t], at(way))

    def from_relay(t):
        return remote(hold.at[lines(t)], near.at[0, lines(t)], e_send.at[2, t], e_recv.at[1, t], at(2))

    def first_sends(t, carry):
        direct_first = jnp.logical_and(lat == 0, even)

        @pl.when(direct_first)
        def _():
            to_west(t).start()

        relay = jnp.logical_and(jnp.logical_not(even), by_relay(t))

        @pl.when(jnp.logical_not(relay))
        def _():
            to_east(t).start()

        @pl.when(relay)
        def _():
            to_relay(t).start()

        @pl.when(jnp.logical_not(direct_first))
        def _():
            to_west(t).start()

        return carry

    def relayed(t, carry):
        @pl.when(jnp.logical_and(parity == 0, by_relay(t)))
        def _():
            to_relay(t).wait_recv()
            from_relay(t).start()

        return carry

    loads[0].wait()
    pl.semaphore_wait(barrier, len(greeted))
    lax.fori_loop(0, 1, first_sends, 0)

    def slot_of(step):
        target = lax.rem(lon + step + bands, bands)
        slot = jnp.int32(0)
        found = jnp.int32(0)
        for j in range(vals.shape[0]):
            hit = cols[0, j] == target
            slot = jnp.where(hit, j, slot)
            found = jnp.where(hit, 1, found)
        return slot, found > 0

    mine = pl.ds(pl.multiple_of(color * share, share), share)
    loads[3].wait()
    for k, step in enumerate((1, 3, -2, -3)):
        slot, found = slot_of(step)
        w_out[k] = jnp.where(found, vals[slot, mine, :], jnp.zeros((share, block), BF16))

    def rows_of(ref, base):
        return [ref[pl.ds(base + j, levels, stride=pieces), :] for j in range(pieces)]

    loads[1].wait()
    loads[2].wait()
    for j, (u, v) in enumerate(zip(rows_of(search_dual, 0), rows_of(search_incr, 0))):
        own_s[:, pl.ds(j * LANES, LANES)] = u
        g_own[0, :, pl.ds(j * LANES, LANES)] = v
        g_own[1, :, pl.ds(j * LANES, LANES)] = u

    ways = (1, -2)
    for k, way in enumerate(ways):
        go(remote(own_s, near_s.at[k], s_send.at[k], s_recv.at[k], at(way)))
        both = pl.ds(2 * k, 2)
        go(remote(w_out.at[both], w_in.at[both, mine], w_send.at[k], w_recv.at[k], at(way)))

    lax.fori_loop(1, 2 * EARLY, first_sends, 0)

    loads[4].wait()
    for c in range(5):
        for j, value in enumerate(rows_of(coefs, c * flat)):
            g_own[2 + c, :, pl.ds(j * LANES, LANES)] = value
    lane = lax.broadcasted_iota(jnp.int32, (levels, LANES), 1)
    lead = g_own[0, :, pl.ds(0, LANES)]
    last = pltpu.roll(g_own[0, :, pl.ds(block - LANES, LANES)], 2, 1)
    for k in range(1, 7):
        chosen = lane // 2 == k
        lead = jnp.where(chosen, pltpu.roll(g_own[k, :, pl.ds(0, LANES)], 2 * k, 1), lead)
        last = jnp.where(chosen, pltpu.roll(g_own[k, :, pl.ds(block - LANES, LANES)], 2 * k + 2, 1), last)
    g_edge[0] = last
    g_edge[1] = lead

    go(remote(g_own, g_lat, g_send.at[0], g_recv.at[0], at(0, True)))

    def edge(side, other):
        n = 1 + 2 * side + other
        way = 1 - 2 * side
        return remote(g_edge.at[side], g_side.at[side, other], g_send.at[n], g_recv.at[n], at(way, other == 1))

    for side in range(2):
        for other in range(2):
            go(edge(side, other))

    for copy in loads[5:]:
        copy.wait()
    resid_sq = jnp.sum(resid_dual[...] ** 2 + resid_obs[...] ** 2 + resid_incr[...] ** 2)
    search_sq = jnp.sum(search_dual[...] ** 2 + search_obs[...] ** 2 + search_incr[...] ** 2)
    first_row = lax.broadcasted_iota(jnp.int32, (8, LANES), 0) == 0
    part[...] = jnp.where(first_row, resid_sq, search_sq)
    part_lon[lon] = part[...]
    for step in range(1, bands):
        go(remote(part, part_lon.at[lon], a_send.at[step], a_recv.at[lon], at(step)))

    for d, step in enumerate((0, -1, 2)):
        slot, found = slot_of(step)
        w_home[d] = jnp.where(found, vals[slot], jnp.zeros((block, block), BF16))
    acc[...] = jnp.zeros_like(acc)

    every = pl.ds(0, WEIGHTS)
    for k in range(2):
        both = pl.ds(2 * k, 2)
        remote(w_out.at[both], w_in.at[both, mine], w_send.at[k], w_recv.at[k], at(0)).wait_recv()
    spot = w_in.at[every, mine]
    for step in range(1, wins):
        go(remote(spot, spot, f_send.at[step], f_recv.at[win], at(0, False, step)))
    lax.fori_loop(0, EARLY, relayed, 0)
    lax.fori_loop(2 * EARLY, 3 * EARLY, first_sends, 0)

    remote(g_own, g_lat, g_send.at[0], g_recv.at[0], at(0)).wait_recv()
    for side in range(2):
        for other in range(2):
            edge(side, other).wait_recv()

    def wide(k, other):
        middle = g_lat if other else g_own
        before = pltpu.roll(g_side[0, other], LANES - 2 - 2 * k, 1)
        after = pltpu.roll(g_side[1, other], (LANES - 2 * k) % LANES, 1)
        return jnp.concatenate([before, middle[k], after], axis=1)

    span = block + 2 * LANES

    def east(x):
        return pltpu.roll(x, span - 1, 1)

    def west(x):
        return pltpu.roll(x, 1, 1)

    here = [wide(k, 0) for k in range(7)]
    over = [wide(k, 1) for k in range(7)]
    south_row = lat == 0
    cross = jnp.where(south_row, here[5], here[6])
    cross_over = jnp.where(south_row, over[6], over[5])

    def forward(v, beyond, c, between):
        return (0.5 + c[2]) * v + c[3] * east(v) + c[4] * west(v) + between * beyond

    def adjoint(u, beyond, c, between):
        return (0.5 + c[2]) * u + west(c[3] * u) + east(c[4] * u) + between * beyond

    once = forward(here[0], over[0], here, cross)
    once_over = forward(over[0], here[0], over, cross_over)
    twice = forward(once, once_over, here, cross)
    back_once = adjoint(here[1], over[1], here, cross_over)
    back_over = adjoint(over[1], here[1], over, cross)
    back_twice = adjoint(back_once, back_over, here, cross_over)
    for j in range(pieces):
        cut = slice((j + 1) * LANES, (j + 2) * LANES)
        moved[0, pl.ds(j, levels, stride=pieces), :] = twice[:, cut]
        moved[1, pl.ds(j, levels, stride=pieces), :] = back_twice[:, cut]
    for k, way in enumerate((1, -1)):
        go(remote(moved.at[k], moved_in.at[k], m_send.at[k], m_recv.at[k], at(0, False, way)))

    for step in range(1, bands):
        source = lax.rem(lon + step, bands)
        remote(part, part_lon.at[source], a_send.at[step], a_recv.at[source], at(0)).wait_recv()
    pair[...] = jnp.sum(part_lon[...], axis=0)
    part_col[color] = pair[...]
    for step in range(1, colors):
        _, where = peer(step)
        go(remote(pair, part_col.at[color], b_send.at[step], b_recv.at[color], where))

    for step in range(1, wins):
        source = lax.rem(win + step, wins)
        remote(spot, spot, f_send.at[step], f_recv.at[source], at(0)).wait_recv()

    def over_lat(w, holder):
        theirs = pl.ds(pl.multiple_of((w * lats + holder) * share, share), share)
        place = w_in.at[every, theirs]
        return remote(place, place, h_send.at[w], h_recv.at[w], at(0, True))

    for w in range(wins):
        go(over_lat(w, lat))
    lax.fori_loop(3 * EARLY, CHUNKS, first_sends, 0)
    for k in range(2):
        remote(own_s, near_s.at[k], s_send.at[k], s_recv.at[k], at(0)).wait_recv()

    def spread_of(t):
        def read(ref, search):
            member = ref[...].astype(F32).reshape(group, levels, block)
            product = (member * search[None]).astype(BF16).reshape(rows, block)
            return member, product

        def weigh(member, terms):
            total = sum(jnp.dot(p, w, preferred_element_type=F32) for p, w in terms)
            return jnp.sum(member * total.reshape(group, levels, block), axis=0)

        member, product = read(ens.at[lines(t)], own_s[...])
        first, first_product = read(near.at[0, lines(t)], near_s[0])
        second, second_product = read(near.at[1, lines(t)], near_s[1])
        acc[0] += weigh(member, ((product, w_home[0]), (first_product, w_home[1]), (second_product, w_home[2])))
        acc[1] += weigh(first, ((product, w_in[0]), (second_product, w_in[1])))
        acc[2] += weigh(second, ((product, w_in[2]), (first_product, w_in[3])))

    def step_of(t, carry):
        @pl.when(jnp.logical_and(t >= EARLY, t < CHUNKS))
        def _():
            relayed(t, 0)

        @pl.when(t == LAG)
        def _():
            for w in range(wins):
                over_lat(w, 1 - lat).wait_recv()

        @pl.when(t >= LAG)
        def _():
            to_west(t - LAG).wait_recv()
            to_east(t - LAG).wait_recv()
            spread_of(t - LAG)

        return carry

    lax.fori_loop(0, CHUNKS + LAG, step_of, 0)

    for k, way in enumerate(ways):
        go(remote(acc.at[1 + k], back.at[k], r_send.at[k], r_recv.at[k], at(-way)))

    for step in range(1, colors):
        source, where = peer(step)
        remote(pair, part_col.at[source], b_send.at[step], b_recv.at[source], where).wait_recv()
    sums = jnp.sum(part_col[...], axis=0)
    alpha = sums[0:1, :] / (sums[1:2, :] + 1e-6)

    out[0] = dual_state[...] + alpha * search_dual[...]
    out[1] = dual_obs[...] + alpha * search_obs[...]
    out[2] = increment[...] + alpha * search_incr[...]
    image_obs = obs_var[...] * search_obs[...] + obs_weight[...] * search_incr[...]
    out[4] = resid_obs[...] - alpha * image_obs
    for k in range(2):
        remote(moved.at[k], moved_in.at[k], m_send.at[k], m_recv.at[k], at(0)).wait_recv()
    later = jnp.where(win < wins - 1, moved_in[1], 0.0)
    image_incr = search_dual[...] - later + obs_weight[...] * search_obs[...]
    out[5] = resid_incr[...] - alpha * image_incr
    prior = jnp.where(win > 0, moved_in[0], 0.0)

    for k in range(2):
        remote(acc.at[1 + k], back.at[k], r_send.at[k], r_recv.at[k], at(0)).wait_recv()
    covar = (acc[0] + back[0] + back[1]) / (members - 1)
    for j in range(pieces):
        covar_flat[pl.ds(j, levels, stride=pieces), :] = covar[:, j * LANES:(j + 1) * LANES]
    image_dual = covar_flat[...] + search_incr[...] - prior
    out[3] = resid_dual[...] - alpha * image_dual

    for copy in started:
        copy.wait_send()

    def sent(t, carry):
        to_west(t).wait_send()
        to_east(t).wait_send()

        @pl.when(jnp.logical_and(parity == 0, by_relay(t)))
        def _():
            from_relay(t).wait_send()

        return carry

    lax.fori_loop(0, CHUNKS, sent, 0)


def local(wins, bands, lats, *args):
    fields = list(args)
    _, members, levels, _, block = args[9].shape
    flat = levels * block // LANES
    for k in (0, 1, 2, 3, 4, 5, 6, 7, 8, 11, 12):
        fields[k] = args[k].reshape(flat, LANES)
    fields[9] = args[9].reshape(members * levels, block)
    fields[10] = args[10].reshape(5 * flat, LANES)
    fields[14] = args[14][0]
    colors = wins * lats
    share = block // colors
    total = members * levels
    vmem = pl.BlockSpec(memory_space=pltpu.VMEM)
    specs = [pl.BlockSpec(memory_space=pl.ANY)] * 15
    specs[13] = pl.BlockSpec(memory_space=pltpu.SMEM)
    dma = pltpu.SemaphoreType.DMA
    pairs = [(3, CHUNKS), (2,), (2,), (wins,), (wins,), (5,), (bands,), (colors,), (2,), (2,)]
    out = pl.pallas_call(
        functools.partial(kernel, (wins, bands, lats, members, levels, block)),
        out_shape=jax.ShapeDtypeStruct((6, flat, LANES), F32),
        in_specs=specs,
        out_specs=vmem,
        scratch_shapes=[
            pltpu.VMEM(fields[k].shape, fields[k].dtype) for k in range(15) if k != 13
        ] + [
            dma((14,)),
            pltpu.VMEM((2, total, block), BF16),
            pltpu.VMEM((total, block), BF16),
            pltpu.VMEM((2, levels, block), F32),
            pltpu.VMEM((levels, block), F32),
            pltpu.VMEM((3, block, block), BF16),
            pltpu.VMEM((WEIGHTS, share, block), BF16),
            pltpu.VMEM((WEIGHTS, block, block), BF16),
            pltpu.VMEM((7, levels, block), F32),
            pltpu.VMEM((7, levels, block), F32),
            pltpu.VMEM((2, levels, LANES), F32),
            pltpu.VMEM((2, 2, levels, LANES), F32),
            pltpu.VMEM((8, LANES), F32),
            pltpu.VMEM((bands, 8, LANES), F32),
            pltpu.VMEM((8, LANES), F32),
            pltpu.VMEM((colors, 8, LANES), F32),
            pltpu.VMEM((2, flat, LANES), F32),
            pltpu.VMEM((2, flat, LANES), F32),
            pltpu.VMEM((3, levels, block), F32),
            pltpu.VMEM((2, levels, block), F32),
            pltpu.VMEM((flat, LANES), F32),
        ] + [dma(shape) for shape in pairs for _ in range(2)],
        compiler_params=pltpu.CompilerParams(
            collective_id=0, has_side_effects=True, vmem_limit_bytes=60 * 1024 * 1024
        ),
    )(*fields)
    return tuple(out[k].reshape(args[0].shape) for k in range(6))


def solution(mesh):
    wins, bands, lats = (mesh.shape[name] for name in ("win", "lon", "lat"))
    field = P("win", None, "lat", "lon")
    deep = P("win", None, None, "lat", "lon")
    return jax.shard_map(
        functools.partial(local, wins, bands, lats),
        mesh=mesh,
        in_specs=(field,) * 9 + (deep, deep, field, field, P("lon", None), P("lon", None, None, None)),
        out_specs=(field,) * 6,
        check_vma=False,
    )
```
